1024 devices in a mesh: seq: 32 (over z, core), exp: 8 (over y), head: 4 (over x).
Axes of the slice: x: 4, y: 8, z: 16, core: 2. Of those that a mesh axis runs over, the one named last changes fastest.
Arguments:
- resid: bfloat16 [4096, 4096], P('seq'), may hold values from -6 to 6
- grad_out: bfloat16 [4096, 4096], P('seq'), may hold values from -6 to 6
- norm_gain: bfloat16 [4096], replicated, may hold values from 0.25 to 1.75
- expert_ids: int32 [4096, 2], P('seq'), may hold values from 0 to 7, all different within a row; in each aligned block of 32 rows (0 to 31, 32 to 63, ...) at most 12 rows name the same one
- route_weights: float32 [4096, 2], P('seq'), may hold values from 0.2 to 1
- w_gate: bfloat16 [8, 4096, 6400], P('exp', None, 'seq'), may hold values from -0.09375 to 0.09375
- w_up: bfloat16 [8, 4096, 6400], P('exp', None, 'seq'), may hold values from -0.09375 to 0.09375
- w_down: bfloat16 [8, 6400, 4096], P('exp', 'seq'), may hold values from -0.078125 to 0.078125
- w_out: bfloat16 [4096, 4096], P(('exp', 'head')), may hold values from -0.09375 to 0.09375
- queries: bfloat16 [4096, 4096], P('seq', ('exp', 'head')), may hold values from -18 to 18
- keys: bfloat16 [4096, 4096], P('seq', ('exp', 'head')), may hold values from -6 to 6
- values: bfloat16 [4096, 4096], P('seq', ('exp', 'head')), may hold values from -6 to 6
Outputs:
- grad_resid: bfloat16 [4096, 4096], P(('seq', 'head'))
- query_grad: bfloat16 [4096, 4096], P('seq', ('exp', 'head'))
The draws below stay inside these ranges and needn't reach their ends.
Inputs may be any that keep to these rules, and one draw needn't show every extreme that they name: `expert_ids`: each row names two different experts. In each aligned block of 32 rows no expert is named by more than 12 rows, a bound that some block reaches.
All inputs are finite; a program needn't handle non-finite values.
Results may differ from the reference program's by a relative error of at most 0.0085.
Values may be sent and summed in bfloat16 or wider, within the bound.
No kernel may reach another device: no remote copies, remote signals or barrier semaphores. Data moves between devices by JAX's collectives and lax.ppermute only.
A program may use at most 64 MiB of HBM per device.

```python
import math
import jax
import jax.numpy as jnp
import numpy as np
from jax import lax

D = 4096
FF = 6400
HEADS = 32
HD = 128
EXPERTS = 8
TOKENS = 4096
QROWS = 32
CAP = 12
N_SEQ = 32
N_HEAD = 4


def drawn_pair(key):
    base = jax.random.fold_in(key, 1913)
    key_q, key_k = jax.random.split(base, 2)
    row_width = HEADS * HD
    query_rows = jnp.clip(jax.random.normal(key_q, (TOKENS, row_width), jnp.float32), -6.0, 6.0)
    key_rows = jnp.clip(jax.random.normal(key_k, (TOKENS, row_width), jnp.float32), -6.0, 6.0)
    return (query_rows, key_rows)


def draw_queries(key, part):
    return drawn_pair(key)[0].astype(jnp.bfloat16)


def draw_keys(key, part):
    return drawn_pair(key)[1].astype(jnp.bfloat16)


def levels(key, dims, pieces, smallest, top_value):
    level, own = 1.0, jax.random.fold_in(key, 6)
    for axis_at, blocks in pieces:
        heights = jnp.exp(jax.random.uniform(jax.random.fold_in(own, axis_at), (blocks,), jnp.float32, smallest / len(pieces), top_value / len(pieces)))
        level = level * jnp.repeat(heights, dims[axis_at] // blocks).reshape([-1 if axis == axis_at else 1 for axis in range(len(dims))])
    return level


def assign_block(own_key, own, number, rows, number_of, top, bound, skew):
    ranking = jax.random.permutation(own_key, number_of)
    heavy_load, usual = portions_of(number_of, rows * top, bound, skew, True), portions_of(number_of, rows * top, bound, skew, False)
    places = jnp.arange(number_of)

    def named(sizes, offset_by):
        used = int((sizes > 0).sum())
        fixed = max(1, used // 4)
        passed = fixed + (places - fixed + offset_by * (used - fixed)) % max(1, number_of - fixed)
        return jnp.zeros((number_of,), jnp.int32).at[ranking[jnp.where(places < fixed, places, passed)]].set(jnp.asarray(sizes, jnp.int32))

    sizes = jnp.where(number % 4 == 0, named(heavy_load, number // 4), named(usual, number - number // 4 - 1))
    mixed = jax.random.permutation(jax.random.fold_in(own, 3), number_of)
    source_of, sink = mixed[0:number_of // 2 * 2:2], mixed[1:number_of // 2 * 2:2]
    slack = jnp.minimum(sizes[source_of] - 1, bound - sizes[sink]) // 2
    slack = jnp.where((source_of == ranking[0]) | (sink == ranking[0]) | (sizes[sink] == 0), 0, jnp.maximum(slack, 0))
    passed = jax.random.randint(jax.random.fold_in(own, 4), (number_of // 2,), 0, 1 << 20) % (slack + 1)
    sizes = sizes.at[source_of].add(-passed).at[sink].add(passed)
    members = jnp.searchsorted(jnp.cumsum(sizes), jnp.arange(rows * top), side="right").astype(jnp.int32)
    grid = members.reshape(top, rows).T
    grid = grid[jax.random.permutation(jax.random.fold_in(own, 1), rows)]
    offset_by = jax.random.randint(jax.random.fold_in(own, 2), (rows, 1), 0, top)
    return jnp.take_along_axis(grid, (jnp.arange(top)[None, :] + offset_by) % top, axis=1)


def portions_of(amount, total, bound, slope, full):
    portions = [(1 << 20) // math.isqrt(standing ** slope) + 1 for standing in range(1, amount + 1)]
    largest = bound if full else min(bound, max(-(-total // amount), total * portions[0] // sum(portions)))
    least = 1 if total - largest >= amount - 1 else 0
    given, rest = [largest] + [least] * (amount - 1), total - largest - least * (amount - 1)
    while rest > 0:
        free = [i for i in range(1, amount) if given[i] < largest] or [i for i in range(1, amount) if given[i] < bound]
        whole, budget = sum([portions[i] for i in free]), rest
        for i in free:
            extra = min(bound - given[i], max(1, budget * portions[i] // whole), rest)
            given[i] = given[i] + extra
            rest = rest - extra
    return np.array(given)


def gaussian(key, extent, deviation, limit, cuts=(), kind=jnp.bfloat16):
    drawn = jax.random.normal(key, extent, jnp.float32) * deviation
    if len(cuts) > 0:
        drawn = levels(key, extent, cuts, -0.22, 0.18) * drawn
    return jnp.clip(drawn, min=-limit, max=limit).astype(kind)


def setup_inputs(seed: int = 0) -> dict:
    key_list = jax.random.split(jax.random.key(seed), 13)
    resid = gaussian(key_list[0], (TOKENS, D), 1.0, 6.0, ((0, 32),))
    grad_out = gaussian(key_list[1], (TOKENS, D), 1.0, 6.0, ((0, 32),))
    norm_gain = jnp.clip(1.0 + 0.15 * jax.random.normal(key_list[2], (D,), jnp.float32), 0.25, 1.75).astype(jnp.bfloat16)
    expert_ids_keys = jax.random.split(jax.random.fold_in(key_list[3], 1), TOKENS // QROWS)
    expert_ids_turns = jax.random.permutation(jax.random.fold_in(key_list[3], 3), TOKENS // QROWS)
    expert_ids = jax.vmap(lambda own, number: assign_block(jax.random.fold_in(key_list[3], 2), own, number, QROWS, EXPERTS, 2, CAP, 2))(expert_ids_keys, expert_ids_turns).reshape((TOKENS, 2))
    route_weights = jnp.clip(0.2 + 0.8 * jax.random.uniform(key_list[4], (TOKENS, 2), jnp.float32) ** levels(key_list[4], (TOKENS, 2), ((0, 32),), -0.2, 0.2), 0.2, 1.0)
    w_gate = gaussian(key_list[5], (EXPERTS, D, FF), D ** -0.5, 0.09375, ((0, 8), (2, 32)))
    w_up = gaussian(key_list[6], (EXPERTS, D, FF), D ** -0.5, 0.09375, ((0, 8), (2, 32)))
    w_down = gaussian(key_list[7], (EXPERTS, FF, D), FF ** -0.5, 0.078125, ((0, 8), (1, 32)))
    w_out = gaussian(key_list[8], (HEADS * HD, D), (HEADS * HD) ** -0.5, 0.09375, ((0, 32),))
    queries = draw_queries(jax.random.fold_in(key_list[12], 71), 0)
    keys = draw_keys(jax.random.fold_in(key_list[12], 71), 0)
    values = gaussian(key_list[11], (TOKENS, HEADS * HD), 1.0, 6.0, ((0, 32), (1, 32)))
    return dict(resid=resid, grad_out=grad_out, norm_gain=norm_gain, expert_ids=expert_ids, route_weights=route_weights, w_gate=w_gate, w_up=w_up, w_down=w_down, w_out=w_out, queries=queries, keys=keys, values=values)


EPSILON = 1e-05

def norm_parts(resid, norm_gain):
    resid_full = resid.astype(jnp.float32)
    inv_rms = lax.rsqrt(lax.optimization_barrier(jnp.mean(resid_full * resid_full, axis=-1, keepdims=True)) + EPSILON)
    normed = (resid_full * inv_rms * norm_gain.astype(jnp.float32)).astype(jnp.bfloat16)
    return (resid_full, inv_rms, normed)

def swiglu_back(rows_in, rows_grad, gate_mat, up_mat, down_mat):
    gate_val = jnp.dot(rows_in, gate_mat, preferred_element_type=jnp.float32)
    up_val = jnp.dot(rows_in, up_mat, preferred_element_type=jnp.float32)
    hidden_grad = lax.dot_general(rows_grad, down_mat, (((1,), (1,)), ((), ())), preferred_element_type=jnp.float32)
    sigma = jax.nn.sigmoid(gate_val)
    gate_grad = (hidden_grad * up_val * sigma * (1.0 + gate_val * (1.0 - sigma))).astype(jnp.bfloat16)
    up_grad = (hidden_grad * gate_val * sigma).astype(jnp.bfloat16)
    return (gate_grad, up_grad)

def rows_back(gate_grad, up_grad, gate_mat, up_mat):
    contract = (((1,), (1,)), ((), ()))
    first_term = lax.dot_general(gate_grad, gate_mat, contract, preferred_element_type=jnp.float32)
    return first_term + lax.dot_general(up_grad, up_mat, contract, preferred_element_type=jnp.float32)

def norm_back(resid_full, inv_rms, grad_rows, norm_gain, expert_grad):
    scaled_grad = norm_gain.astype(jnp.float32) * expert_grad
    cubed = inv_rms * inv_rms * inv_rms
    mean_term = lax.optimization_barrier(jnp.mean(scaled_grad * resid_full, axis=-1, keepdims=True))
    return (grad_rows.astype(jnp.float32) + inv_rms * scaled_grad - resid_full * cubed * mean_term).astype(jnp.bfloat16)

def reference(resid, grad_out, norm_gain, expert_ids, route_weights, w_gate, w_up, w_down, w_out, queries, keys, values):
    resid_full, inv_rms, normed = norm_parts(resid, norm_gain)
    grad_full = grad_out.astype(jnp.float32)
    most_rows = N_SEQ * N_HEAD * CAP
    row_ids = jnp.arange(most_rows)

    def add_expert(expert, total):
        matched = expert_ids == expert
        routed = jnp.any(matched, axis=1)
        weight = lax.optimization_barrier(jnp.sum(jnp.where(matched, route_weights, 0.0), axis=1))
        picked = jnp.nonzero(routed, size=most_rows, fill_value=0)[0].astype(jnp.int32)
        live = (row_ids < jnp.sum(routed.astype(jnp.int32))).astype(jnp.float32)
        rows_in = normed[picked]
        rows_grad = (weight[picked][:, None] * grad_full[picked]).astype(jnp.bfloat16)
        gate_grad, up_grad = swiglu_back(rows_in, rows_grad, w_gate[expert], w_up[expert], w_down[expert])
        back = rows_back(gate_grad, up_grad, w_gate[expert], w_up[expert])
        return total.at[picked].add(back * live[:, None])
    expert_grad = lax.fori_loop(0, EXPERTS, add_expert, jnp.zeros((TOKENS, D), jnp.float32))
    grad_resid = norm_back(resid_full, inv_rms, grad_out, norm_gain, expert_grad)
    attn_grad = lax.dot_general(grad_resid, w_out, (((1,), (1,)), ((), ())), preferred_element_type=jnp.float32).astype(jnp.bfloat16)
    scale = HD ** (-0.5)
    positions = jnp.arange(TOKENS)
    allowed = positions[None, :] <= positions[:, None]

    def per_head(stacked):
        head_q, head_k, head_v, head_do = stacked
        scores = jnp.dot(head_q, head_k.T, preferred_element_type=jnp.float32) * scale
        scores = jnp.where(allowed, scores, -1e+30)
        row_max = lax.optimization_barrier(jnp.max(scores, axis=-1, keepdims=True))
        expo_vals = jnp.where(allowed, jnp.exp(scores - row_max), 0.0)
        probs = expo_vals / lax.optimization_barrier(jnp.sum(expo_vals, axis=-1, keepdims=True))
        output = jnp.dot(probs, head_v.astype(jnp.float32), precision=lax.Precision.HIGHEST)
        delta = lax.optimization_barrier(jnp.sum(head_do.astype(jnp.float32) * output, axis=-1, keepdims=True))
        prob_grad = jnp.dot(head_do, head_v.T, preferred_element_type=jnp.float32)
        mixed = probs * (prob_grad - delta)
        return (scale * jnp.dot(mixed, head_k.astype(jnp.float32), precision=lax.Precision.HIGHEST)).astype(jnp.bfloat16)

    def by_head(array):
        return array.reshape(TOKENS, HEADS, HD).transpose(1, 0, 2)
    per_heads = lax.map(per_head, (by_head(queries), by_head(keys), by_head(values), by_head(attn_grad)))
    query_grad = per_heads.transpose(1, 0, 2).reshape(TOKENS, HEADS * HD)
    return (grad_resid, query_grad)
```

```python
import jax
import jax.numpy as jnp
from jax import lax
from jax.sharding import PartitionSpec as P

HD = 128


EPSILON = 1e-05


def norm_back(resid_rows, grad_rows, norm_gain, expert_grad):
    resid_full = resid_rows.astype(jnp.float32)
    inv_rms = lax.rsqrt(jnp.mean(resid_full * resid_full, axis=-1, keepdims=True) + EPSILON)
    scaled_grad = norm_gain.astype(jnp.float32) * expert_grad
    cubed = inv_rms * inv_rms * inv_rms
    mean_term = jnp.mean(scaled_grad * resid_full, axis=-1, keepdims=True)
    return (
        grad_rows.astype(jnp.float32) + inv_rms * scaled_grad - resid_full * cubed * mean_term
    ).astype(jnp.bfloat16)


def per_device(
    resid,
    grad_out,
    norm_gain,
    expert_ids,
    route_weights,
    w_gate,
    w_up,
    w_down,
    w_out,
    queries,
    keys,
    values,
):
    tok_rows = resid.shape[0]
    width = resid.shape[1]
    head_count = lax.axis_size("head")
    exp_count = lax.axis_size("exp")
    quarter = tok_rows // head_count
    local_experts = w_gate.shape[0]
    capacity = 3 * quarter // (local_experts * exp_count)
    seq_index = lax.axis_index("seq")
    exp_index = lax.axis_index("exp")
    head_index = lax.axis_index("head")
    row_first = head_index * quarter
    resid_part = lax.dynamic_slice_in_dim(resid, row_first, quarter, 0)
    grad_part = lax.dynamic_slice_in_dim(grad_out, row_first, quarter, 0)
    ids_part = lax.dynamic_slice_in_dim(expert_ids, row_first, quarter, 0)
    weights_part = lax.dynamic_slice_in_dim(route_weights, row_first, quarter, 0)
    resid_full = resid_part.astype(jnp.float32)
    inv_rms = lax.rsqrt(jnp.mean(resid_full * resid_full, axis=-1, keepdims=True) + EPSILON)
    normed = (resid_full * inv_rms * norm_gain.astype(jnp.float32)).astype(jnp.bfloat16)
    grad_full = grad_part.astype(jnp.float32)
    slot_ids = lax.broadcasted_iota(jnp.int32, (capacity, quarter), 0)
    contract = (((1,), (1,)), ((), ()))
    expert = exp_index * local_experts + 0
    matched = ids_part == expert
    routed = jnp.any(matched, axis=1)
    weight = jnp.sum(jnp.where(matched, weights_part, 0.0), axis=1)
    row_ids = jnp.arange(quarter, dtype=jnp.int32)
    earlier = row_ids[:, None] < row_ids[None, :]
    position = jnp.sum((earlier & routed[:, None]).astype(jnp.int32), axis=0)
    select = (position[None, :] == slot_ids) & routed[None, :]
    select_mat = select.astype(jnp.bfloat16)
    slot_in = jnp.dot(select_mat, normed, preferred_element_type=jnp.float32).astype(jnp.bfloat16)
    scaled = (weight[:, None] * grad_full).astype(jnp.bfloat16)
    slot_grad = jnp.dot(select_mat, scaled, preferred_element_type=jnp.float32).astype(jnp.bfloat16)
    gate_mat = w_gate[0]
    up_mat = w_up[0]
    down_mat = w_down[0]
    rows_in = lax.all_gather(slot_in, "seq", axis=0, tiled=True)
    rows_grad = lax.all_gather(slot_grad, "seq", axis=0, tiled=True)
    gate_val = jnp.dot(rows_in, gate_mat, preferred_element_type=jnp.float32)
    up_val = jnp.dot(rows_in, up_mat, preferred_element_type=jnp.float32)
    hidden_grad = lax.dot_general(rows_grad, down_mat, contract, preferred_element_type=jnp.float32)
    sigma = jax.nn.sigmoid(gate_val)
    gate_grad = (hidden_grad * up_val * sigma * (1.0 + gate_val * (1.0 - sigma))).astype(
        jnp.bfloat16
    )
    up_grad = (hidden_grad * gate_val * sigma).astype(jnp.bfloat16)
    all_slots = lax.dot_general(gate_grad, gate_mat, contract, preferred_element_type=jnp.float32)
    all_slots = all_slots + lax.dot_general(
        up_grad, up_mat, contract, preferred_element_type=jnp.float32
    )
    slots_back = lax.psum_scatter(all_slots, "seq", scatter_dimension=0, tiled=True)
    local_sum = jnp.dot(select.astype(jnp.float32).T, slots_back, precision=lax.Precision.HIGHEST)
    share = quarter // exp_count
    summed = lax.psum_scatter(local_sum, "exp", scatter_dimension=0, tiled=True)
    share_first = exp_index * share
    resid_share = lax.dynamic_slice_in_dim(resid_part, share_first, share, 0)
    grad_share_in = lax.dynamic_slice_in_dim(grad_part, share_first, share, 0)
    grad_share = norm_back(resid_share, grad_share_in, norm_gain, summed)
    gathered = lax.all_gather(grad_share, ("exp", "head"), axis=0, tiled=True)
    full_grad = (
        gathered.reshape(exp_count, head_count, share, width)
        .transpose(1, 0, 2, 3)
        .reshape(tok_rows, width)
    )
    grad_quarter = lax.dynamic_slice_in_dim(full_grad, row_first, quarter, 0)
    heads_here = queries.shape[1] // HD
    attn_grad = lax.dot_general(
        full_grad, w_out, contract, preferred_element_type=jnp.float32
    ).astype(jnp.bfloat16)
    query_three = queries.reshape(tok_rows, heads_here, HD)
    attn_three = attn_grad.reshape(tok_rows, heads_here, HD)
    query_pos = seq_index * tok_rows + jnp.arange(tok_rows, dtype=jnp.int32)
    scale = HD ** (-0.5)
    highest = lax.Precision.HIGHEST
    start_max = jnp.full((heads_here, tok_rows), -1e30, jnp.float32)
    run_max = start_max
    key_piece = lax.all_gather(keys, "seq", axis=0, tiled=True)
    value_piece = lax.all_gather(values, "seq", axis=0, tiled=True)
    key_count = key_piece.shape[0]
    key_three = key_piece.reshape(key_count, heads_here, HD)
    value_three = value_piece.reshape(key_count, heads_here, HD)
    scores = (
        jnp.einsum("qhd,khd->hqk", query_three, key_three, preferred_element_type=jnp.float32)
        * scale
    )
    key_pos = jnp.arange(key_count, dtype=jnp.int32)
    allowed = (key_pos[None, :] <= query_pos[:, None])[None, :, :]
    scores = jnp.where(allowed, scores, -1e30)
    new_max = jnp.maximum(run_max, jnp.max(scores, axis=-1))
    expo_vals = jnp.where(allowed, jnp.exp(scores - new_max[:, :, None]), 0.0)
    prob_grad = jnp.einsum(
        "qhd,khd->hqk", attn_three, value_three, preferred_element_type=jnp.float32
    )
    key_full = key_three.astype(jnp.float32)
    value_full = value_three.astype(jnp.float32)
    run_sum = jnp.sum(expo_vals, axis=-1)
    acc_val = jnp.einsum("hqk,khd->hqd", expo_vals, value_full, precision=highest)
    acc_mix = jnp.einsum("hqk,khd->hqd", expo_vals * prob_grad, key_full, precision=highest)
    acc_key = jnp.einsum("hqk,khd->hqd", expo_vals, key_full, precision=highest)
    run_max, run_sum, acc_val, acc_mix, acc_key = (new_max, run_sum, acc_val, acc_mix, acc_key)
    output = acc_val / run_sum[:, :, None]
    attn_heads = attn_three.astype(jnp.float32).transpose(1, 0, 2)
    delta = jnp.sum(attn_heads * output, axis=-1, keepdims=True)
    query_heads = scale * (acc_mix - delta * acc_key) / run_sum[:, :, None]
    query_grad = (
        query_heads.transpose(1, 0, 2).reshape(tok_rows, heads_here * HD).astype(jnp.bfloat16)
    )
    return (grad_quarter, query_grad)


def solution(mesh):
    in_specs = (
        P("seq", None),
        P("seq", None),
        P(),
        P("seq", None),
        P("seq", None),
        P("exp", None, "seq"),
        P("exp", None, "seq"),
        P("exp", "seq", None),
        P(("exp", "head"), None),
        P("seq", ("exp", "head")),
        P("seq", ("exp", "head")),
        P("seq", ("exp", "head")),
    )
    out_specs = (P(("seq", "head"), None), P("seq", ("exp", "head")))
    return jax.shard_map(
        per_device, mesh=mesh, in_specs=in_specs, out_specs=out_specs, check_vma=False
    )
```

```python
import jax
import jax.numpy as jnp
from jax import lax
from jax.sharding import Mesh, PartitionSpec as P

HD = 128
EPSILON = 1e-05
CAP = 12
FOLD = 4

CONTRACT = (((1,), (1,)), ((), ()))


def spread(rows, axis, size, dist):
    up = [(a, (a + dist) % size) for a in range(size)]
    down = [(a, (a - dist) % size) for a in range(size)]
    if axis == "z":
        pairs = [(2 * a, 2 * b) for a, b in up] + [(2 * a + 1, 2 * b + 1) for a, b in down]
        return lax.ppermute(rows, ("z", "core"), pairs)
    pairs = up + [(size + a, size + b) for a, b in down]
    return lax.ppermute(rows, ("core", axis), pairs)


def core_swap(block):
    return lax.ppermute(block, "core", [(0, 1), (1, 0)])


def norm_back(resid_full, inv_rms, grad_rows, norm_gain, expert_grad):
    scaled_grad = norm_gain.astype(jnp.float32) * expert_grad
    cubed = inv_rms * inv_rms * inv_rms
    mean_term = jnp.mean(scaled_grad * resid_full, axis=-1, keepdims=True)
    return (grad_rows + inv_rms * scaled_grad - resid_full * cubed * mean_term).astype(jnp.bfloat16)


def per_device(
    resid,
    grad_out,
    norm_gain,
    expert_ids,
    route_weights,
    w_gate,
    w_up,
    w_down,
    w_out,
    queries,
    keys,
    values,
):
    f32, bf16 = jnp.float32, jnp.bfloat16
    tok_rows, width = resid.shape
    z_count, exp_count, head_count = (lax.axis_size(a) for a in ("z", "exp", "head"))
    z_index, core_index = lax.axis_index("z"), lax.axis_index("core")
    exp_index, head_index = lax.axis_index("exp"), lax.axis_index("head")
    quarter = tok_rows // head_count
    row_first = head_index * quarter
    resid_part = lax.dynamic_slice_in_dim(resid, row_first, quarter, 0)
    grad_part = lax.dynamic_slice_in_dim(grad_out, row_first, quarter, 0)
    ids_part = lax.dynamic_slice_in_dim(expert_ids, row_first, quarter, 0)
    weights_part = lax.dynamic_slice_in_dim(route_weights, row_first, quarter, 0)
    resid_full = resid_part.astype(f32)
    inv_rms = lax.rsqrt(jnp.mean(resid_full * resid_full, axis=-1, keepdims=True) + EPSILON)
    normed = (resid_full * inv_rms * norm_gain.astype(f32)).astype(bf16)
    grad_full = grad_part.astype(f32)

    row_ids = jnp.arange(quarter, dtype=jnp.int32)
    earlier = row_ids[:, None] < row_ids[None, :]

    def slots_of(expert):
        matched = ids_part == expert
        routed = jnp.any(matched, axis=1)
        position = jnp.sum((earlier & routed[:, None]).astype(jnp.int32), axis=0)
        weight = jnp.sum(jnp.where(matched, weights_part, 0.0), axis=1)
        return routed, position, weight

    routed, position, weight = slots_of(exp_index)
    slot_ids = jnp.arange(CAP, dtype=jnp.int32)
    select = ((position[None, :] == slot_ids[:, None]) & routed[None, :]).astype(bf16)
    scaled = (weight[:, None] * grad_full).astype(bf16)
    slot_in = jnp.dot(select, normed, preferred_element_type=f32).astype(bf16)
    slot_grad = jnp.dot(select, scaled, preferred_element_type=f32).astype(bf16)
    mine = jnp.concatenate([slot_in, slot_grad], axis=0)

    rows = lax.all_gather(mine, "z", axis=0, tiled=True)
    gate_mat, up_mat, down_mat, w_mine, mine = lax.optimization_barrier(
        (w_gate[0].T, w_up[0].T, w_down[0], w_out, mine)
    )
    gate_two = jnp.concatenate([gate_mat, core_swap(gate_mat)], axis=0)
    up_two = jnp.concatenate([up_mat, core_swap(up_mat)], axis=0)
    down_two = jnp.concatenate([down_mat, core_swap(down_mat)], axis=0)
    w_near = [w_mine] + [
        lax.ppermute(w_mine, "head", [(a, (a - d) % head_count) for a in range(head_count)])
        for d in range(1, head_count)
    ]
    w_four = jnp.concatenate(w_near, axis=0)

    units = gate_two.shape[0]
    gate_all = lax.dot_general(rows, gate_two, CONTRACT, preferred_element_type=f32)
    up_all = lax.dot_general(rows, up_two, CONTRACT, preferred_element_type=f32)
    down_all = lax.dot_general(rows, down_two, CONTRACT, preferred_element_type=f32)
    gate_val = gate_all.reshape(z_count, 2 * CAP, units)[:, :CAP].reshape(-1, units)
    up_val = up_all.reshape(z_count, 2 * CAP, units)[:, :CAP].reshape(-1, units)
    hidden_grad = down_all.reshape(z_count, 2 * CAP, units)[:, CAP:].reshape(-1, units)
    sigma = jax.nn.sigmoid(gate_val)
    gate_grad = (hidden_grad * up_val * sigma * (1.0 + gate_val * (1.0 - sigma))).astype(bf16)
    up_grad = (hidden_grad * gate_val * sigma).astype(bf16)
    back = jnp.dot(gate_grad, gate_two, preferred_element_type=f32)
    back = back + jnp.dot(up_grad, up_two, preferred_element_type=f32)

    pair, rows = lax.optimization_barrier((jnp.concatenate([keys, values], axis=1), rows))
    pair_here = lax.all_gather(pair, "z", axis=0, tiled=True)
    pair_all = jnp.concatenate([pair_here, core_swap(pair_here)], axis=0)
    key_all, value_all = pair_all[:, :HD], pair_all[:, HD:]

    part = width // FOLD
    left = back.reshape(z_count, CAP, FOLD, part).transpose(0, 2, 1, 3)
    left = left.reshape(z_count, FOLD * CAP, part)
    dist = 1
    while dist < z_count:
        bit = (z_index // dist) % 2
        two = left.reshape(left.shape[0] // 2, 2, FOLD * CAP, part)
        stay = lax.dynamic_index_in_dim(two, bit, 1, keepdims=False)
        leave = lax.dynamic_index_in_dim(two, 1 - bit, 1, keepdims=False).astype(bf16)
        left = stay + spread(leave, "z", z_count, dist).astype(f32)
        dist *= 2
    slots = left.astype(bf16)
    offsets = [0]
    dist = exp_count // 2
    while dist >= 1:
        slots = jnp.concatenate([slots, spread(slots, "exp", exp_count, dist)], axis=0)
        offsets = offsets + [o + dist for o in offsets]
        dist //= 2
    toward = jnp.where(core_index == 0, -1, 1)
    picks = []
    for offset in offsets:
        routed, position, _ = slots_of((exp_index + toward * offset + exp_count) % exp_count)
        picks.append((position[:, None] == slot_ids[None, :]) & routed[:, None])
    picks = jnp.stack(picks, axis=1).astype(bf16)
    flat = slots.reshape(exp_count * FOLD * CAP, part)
    pieces = []
    for q in range(FOLD):
        there = jnp.zeros((quarter, exp_count, FOLD, CAP), bf16).at[:, :, q].set(picks)
        pieces.append(jnp.dot(there.reshape(quarter, -1), flat, preferred_element_type=f32))
    summed = jnp.concatenate(pieces, axis=1)
    grad_quarter = norm_back(resid_full, inv_rms, grad_full, norm_gain, summed)

    at_heads = lax.dot_general(grad_quarter, w_four, CONTRACT, preferred_element_type=f32)
    at_heads = at_heads.astype(bf16)
    pieces = [at_heads[:, :HD]] + [
        lax.ppermute(
            at_heads[:, d * HD : (d + 1) * HD],
            "head",
            [(a, (a + d) % head_count) for a in range(head_count)],
        )
        for d in range(1, head_count)
    ]
    stacked = jnp.stack(pieces[::-1] + pieces[::-1], axis=0).reshape(-1, HD)
    attn_grad = lax.dynamic_slice_in_dim(
        stacked, (head_count - 1 - head_index) * quarter, head_count * quarter, 0
    )

    scale = HD ** (-0.5)
    highest = lax.Precision.HIGHEST
    query_pos = (z_index * 2 + core_index) * tok_rows + jnp.arange(tok_rows, dtype=jnp.int32)
    place = jnp.arange(2 * z_count * tok_rows, dtype=jnp.int32)
    half = z_count * tok_rows
    shard = (place % half) // tok_rows * 2 + (core_index + place // half) % 2
    key_pos = shard * tok_rows + place % tok_rows
    allowed = key_pos[None, :] <= query_pos[:, None]
    scores = lax.dot_general(queries, key_all, CONTRACT, preferred_element_type=f32) * scale
    scores = jnp.where(allowed, scores, -1e30)
    row_max = jnp.max(scores, axis=-1, keepdims=True)
    expo_vals = jnp.where(allowed, jnp.exp(scores - row_max), 0.0)
    probs = expo_vals / jnp.sum(expo_vals, axis=-1, keepdims=True)
    output = jnp.dot(probs, value_all.astype(f32), precision=highest)
    delta = jnp.sum(attn_grad.astype(f32) * output, axis=-1, keepdims=True)
    prob_grad = lax.dot_general(attn_grad, value_all, CONTRACT, preferred_element_type=f32)
    mixed = probs * (prob_grad - delta)
    query_grad = (scale * jnp.dot(mixed, key_all.astype(f32), precision=highest)).astype(bf16)
    return (grad_quarter, query_grad)


def solution(mesh):
    seq, exp, head = mesh.shape["seq"], mesh.shape["exp"], mesh.shape["head"]
    fine = Mesh(mesh.devices.reshape(seq // 2, 2, exp, head), ("z", "core", "exp", "head"))
    seq_axes = ("z", "core")
    in_specs = (
        P(seq_axes, None),
        P(seq_axes, None),
        P(),
        P(seq_axes, None),
        P(seq_axes, None),
        P("exp", None, seq_axes),
        P("exp", None, seq_axes),
        P("exp", seq_axes, None),
        P(("exp", "head"), None),
        P(seq_axes, ("exp", "head")),
        P(seq_axes, ("exp", "head")),
        P(seq_axes, ("exp", "head")),
    )
    out_specs = (P(("z", "core", "head"), None), P(seq_axes, ("exp", "head")))
    return jax.shard_map(
        per_device, mesh=fine, in_specs=in_specs, out_specs=out_specs, check_vma=False
    )
```

```python
import functools

import jax
import jax.numpy as jnp
from jax import lax
from jax.experimental import pallas as pl
from jax.experimental.pallas import tpu as pltpu
from jax.sharding import Mesh, PartitionSpec as P

HD = 128
EPSILON = 1e-05
CAP = 12
FOLD = 4
ROOM = 16
UNITS = 256
MIB = 2**20

CONTRACT = (((1,), (1,)), ((), ()))


def across(left, right):
    return lax.dot_general(left, right, CONTRACT, preferred_element_type=jnp.float32)


def two_terms(full):
    high = full.astype(jnp.bfloat16)
    return high, (full - high.astype(jnp.float32)).astype(jnp.bfloat16)


def expert_kernel(bit_ref, rows_ref, w_ref, stay_ref, leave_ref, back_ref):
    step = pl.program_id(0)
    shards, _, width = rows_ref.shape
    part = width // FOLD
    ins = rows_ref[:, :ROOM, :].reshape(shards * ROOM, width)
    grads = rows_ref[:, ROOM:, :].reshape(shards * ROOM, width)
    gate_val = across(ins, w_ref[0, 0])
    up_val = across(ins, w_ref[0, 1])
    hidden_grad = across(grads, w_ref[0, 2])
    sigma = jax.nn.sigmoid(gate_val)
    gate_grad = (hidden_grad * up_val * sigma * (1.0 + gate_val * (1.0 - sigma))).astype(jnp.bfloat16)
    up_grad = (hidden_grad * gate_val * sigma).astype(jnp.bfloat16)
    for q in range(FOLD):
        at = slice(q * part, (q + 1) * part)
        piece = jnp.dot(gate_grad, w_ref[0, 0, :, at], preferred_element_type=jnp.float32)
        piece = piece + jnp.dot(up_grad, w_ref[0, 1, :, at], preferred_element_type=jnp.float32)
        piece = piece.reshape(shards, ROOM, part)

        @pl.when(step == 0)
        def _():
            back_ref[:, :, at] = piece

        @pl.when(step == 1)
        def _():
            back_ref[:, :, at] += piece

    @pl.when(step == 1)
    def _():
        bit = bit_ref[0]

        def folded(shard):
            block = back_ref[shard]
            return jnp.concatenate([block[:CAP, q * part : (q + 1) * part] for q in range(FOLD)], axis=0)

        for k in range(shards // 2):
            stay_ref[k] = folded(2 * k + bit)
            leave_ref[k] = folded(2 * k + 1 - bit).astype(jnp.bfloat16)


def expert_block(bit, rows, weights):
    shards, depth, width = rows.shape
    out = (shards // 2, FOLD * CAP, width // FOLD)
    return pl.pallas_call(
        expert_kernel,
        grid=(2,),
        in_specs=[
            pl.BlockSpec(memory_space=pltpu.SMEM),
            pl.BlockSpec((shards, depth, width), lambda i: (0, 0, 0)),
            pl.BlockSpec((1, 3, UNITS, width), lambda i: (i, 0, 0, 0)),
        ],
        out_specs=[pl.BlockSpec(out, lambda i: (0, 0, 0))] * 2,
        out_shape=[
            jax.ShapeDtypeStruct(out, jnp.float32),
            jax.ShapeDtypeStruct(out, jnp.bfloat16),
        ],
        scratch_shapes=[pltpu.VMEM((shards, ROOM, width), jnp.float32)],
        compiler_params=pltpu.CompilerParams(vmem_limit_bytes=48 * MIB),
        cost_estimate=pl.CostEstimate(
            flops=2 * 5 * shards * ROOM * 2 * UNITS * width,
            bytes_accessed=2 * weights.size + 2 * rows.size,
            transcendentals=0,
        ),
        name="expert_block",
    )(bit, rows, weights)


def early_kernel(scale, query_ref, key_ref, value_ref, qpos_ref, kpos_ref, prob_ref, out_ref):
    allowed = kpos_ref[...] <= qpos_ref[...]
    scores = jnp.where(allowed, across(query_ref[...], key_ref[...]) * scale, -1e30)
    row_max = jnp.max(scores, axis=-1, keepdims=True)
    expo_vals = jnp.where(allowed, jnp.exp(scores - row_max), 0.0)
    probs = expo_vals / jnp.sum(expo_vals, axis=-1, keepdims=True)
    prob_ref[...] = probs
    high, low = two_terms(probs)
    values = value_ref[...]
    out_ref[...] = jnp.dot(high, values, preferred_element_type=jnp.float32) + jnp.dot(
        low, values, preferred_element_type=jnp.float32
    )


def late_kernel(scale, grad_ref, key_ref, value_ref, prob_ref, out_ref, back_ref):
    grads = grad_ref[...]
    delta = jnp.sum(grads.astype(jnp.float32) * out_ref[...], axis=-1, keepdims=True)
    mixed = prob_ref[...] * (across(grads, value_ref[...]) - delta)
    high, low = two_terms(mixed)
    keys = key_ref[...]
    total = jnp.dot(high, keys, preferred_element_type=jnp.float32) + jnp.dot(
        low, keys, preferred_element_type=jnp.float32
    )
    back_ref[...] = (scale * total).astype(jnp.bfloat16)


def in_vmem(kernel, out_shape, name, flops, *args):
    return pl.pallas_call(
        kernel,
        in_specs=[pl.BlockSpec(memory_space=pltpu.VMEM)] * len(args),
        out_specs=jax.tree.map(lambda _: pl.BlockSpec(memory_space=pltpu.VMEM), out_shape),
        out_shape=out_shape,
        compiler_params=pltpu.CompilerParams(vmem_limit_bytes=32 * MIB),
        cost_estimate=pl.CostEstimate(flops=flops, bytes_accessed=4 * MIB, transcendentals=0),
        name=name,
    )(*args)


def core_swap(block):
    return lax.ppermute(block, "core", [(0, 1), (1, 0)])


def norm_back(resid_full, inv_rms, grad_rows, norm_gain, expert_grad):
    scaled_grad = norm_gain.astype(jnp.float32) * expert_grad
    cubed = inv_rms * inv_rms * inv_rms
    mean_term = jnp.mean(scaled_grad * resid_full, axis=-1, keepdims=True)
    return (grad_rows + inv_rms * scaled_grad - resid_full * cubed * mean_term).astype(jnp.bfloat16)


def per_device(
    resid,
    grad_out,
    norm_gain,
    expert_ids,
    route_weights,
    w_gate,
    w_up,
    w_down,
    w_out,
    queries,
    keys,
    values,
):
    f32, bf16 = jnp.float32, jnp.bfloat16
    tok_rows, width = resid.shape
    z_count, exp_count, head_count = (lax.axis_size(a) for a in ("z", "exp", "head"))
    z_index, core_index = lax.axis_index("z"), lax.axis_index("core")
    exp_index, head_index = lax.axis_index("exp"), lax.axis_index("head")
    quarter = tok_rows // head_count
    row_first = head_index * quarter
    resid_part = lax.dynamic_slice_in_dim(resid, row_first, quarter, 0)
    grad_part = lax.dynamic_slice_in_dim(grad_out, row_first, quarter, 0)
    ids_part = lax.dynamic_slice_in_dim(expert_ids, row_first, quarter, 0)
    weights_part = lax.dynamic_slice_in_dim(route_weights, row_first, quarter, 0)
    resid_full = resid_part.astype(f32)
    inv_rms = lax.rsqrt(jnp.mean(resid_full * resid_full, axis=-1, keepdims=True) + EPSILON)
    normed = (resid_full * inv_rms * norm_gain.astype(f32)).astype(bf16)
    grad_full = grad_part.astype(f32)

    row_ids = jnp.arange(quarter, dtype=jnp.int32)
    earlier = row_ids[:, None] < row_ids[None, :]

    def slots_of(expert):
        matched = ids_part == expert
        routed = jnp.any(matched, axis=1)
        position = jnp.sum((earlier & routed[:, None]).astype(jnp.int32), axis=0)
        weight = jnp.sum(jnp.where(matched, weights_part, 0.0), axis=1)
        return routed, position, weight

    routed, position, weight = slots_of(exp_index)
    slot_ids = jnp.arange(ROOM, dtype=jnp.int32)
    select = ((position[None, :] == slot_ids[:CAP, None]) & routed[None, :]).astype(bf16)
    scaled = (weight[:, None] * grad_full).astype(bf16)
    slot_in = jnp.dot(select, normed, preferred_element_type=f32).astype(bf16)
    slot_grad = jnp.dot(select, scaled, preferred_element_type=f32).astype(bf16)
    spare = ROOM - CAP
    mine = jnp.concatenate(
        [slot_in, keys.reshape(spare, -1), slot_grad, values.reshape(spare, -1)], axis=0
    )

    rows = lax.all_gather(mine, "z", axis=0, tiled=True).reshape(z_count, 2 * ROOM, width)
    gate_mat, up_mat, down_mat, w_mine, mine = lax.optimization_barrier(
        (w_gate[0].T, w_up[0].T, w_down[0], w_out, mine)
    )
    fill = ((0, UNITS - gate_mat.shape[0]), (0, 0))
    own = jnp.stack([jnp.pad(w, fill) for w in (gate_mat, up_mat, down_mat)], axis=0)
    weights = jnp.stack([own, core_swap(own)], axis=0)
    w_near = [w_mine] + [
        lax.ppermute(w_mine, "head", [(a, (a - d) % head_count) for a in range(head_count)])
        for d in range(1, head_count)
    ]
    w_four = jnp.concatenate(w_near, axis=0)
    weights, w_four = lax.optimization_barrier((weights, w_four))

    packed = rows.reshape(z_count, 2, ROOM, width)[:, :, CAP:]
    packed = jnp.stack([packed, core_swap(packed)], axis=0)
    key_all = packed[:, :, 0].reshape(-1, HD)
    value_all = packed[:, :, 1].reshape(-1, HD)
    query_pos = (z_index * 2 + core_index) * tok_rows + jnp.arange(tok_rows, dtype=jnp.int32)
    place = jnp.arange(2 * z_count * tok_rows, dtype=jnp.int32)
    half = z_count * tok_rows
    shard = (place % half) // tok_rows * 2 + (core_index + place // half) % 2
    key_pos = shard * tok_rows + place % tok_rows
    scale = HD ** (-0.5)
    attn_flops = 2 * tok_rows * HD * 2 * half
    probs, output = in_vmem(
        functools.partial(early_kernel, scale),
        [
            jax.ShapeDtypeStruct((tok_rows, 2 * half), f32),
            jax.ShapeDtypeStruct((tok_rows, HD), f32),
        ],
        "attention_early",
        3 * attn_flops,
        queries,
        key_all,
        value_all,
        query_pos[:, None],
        key_pos[None, :],
    )

    bit = z_index % 2
    stay, leave = expert_block(bit.reshape(1), rows, weights)
    up = [(2 * a, 2 * ((a + 1) % z_count)) for a in range(z_count)]
    down = [(2 * a + 1, 2 * ((a - 1) % z_count) + 1) for a in range(z_count)]
    came = lax.ppermute(leave, ("z", "core"), up + down)
    left = (stay + came.astype(f32)).astype(bf16)
    same = [list(range(r, z_count, 2)) for r in range(2)]
    left = lax.all_to_all(left, "z", 0, 0, tiled=True, axis_index_groups=same)
    slots = jnp.sum(left.astype(f32), axis=0).astype(bf16)
    slots = lax.all_to_all(
        jnp.broadcast_to(slots[None], (exp_count, *slots.shape)), "exp", 0, 0, tiled=True
    )
    picks = []
    for expert in range(exp_count):
        routed, position, _ = slots_of(expert)
        picks.append((position[:, None] == slot_ids[None, :CAP]) & routed[:, None])
    picks = jnp.stack(picks, axis=1).astype(bf16)
    flat = slots.reshape(exp_count * FOLD * CAP, -1)
    pieces = []
    for q in range(FOLD):
        there = jnp.zeros((quarter, exp_count, FOLD, CAP), bf16).at[:, :, q].set(picks)
        pieces.append(jnp.dot(there.reshape(quarter, -1), flat, preferred_element_type=f32))
    summed = jnp.concatenate(pieces, axis=1)
    grad_quarter = norm_back(resid_full, inv_rms, grad_full, norm_gain, summed)

    at_heads = lax.dot_general(grad_quarter, w_four, CONTRACT, preferred_element_type=f32)
    at_heads = at_heads.astype(bf16).reshape(quarter, head_count, HD).transpose(1, 0, 2)
    at_heads = jnp.roll(at_heads, head_index, axis=0)
    attn_grad = lax.all_to_all(at_heads, "head", 0, 0, tiled=True).reshape(tok_rows, HD)
    query_grad = in_vmem(
        functools.partial(late_kernel, scale),
        jax.ShapeDtypeStruct((tok_rows, HD), bf16),
        "attention_late",
        3 * attn_flops,
        attn_grad,
        key_all,
        value_all,
        probs,
        output,
    )
    return (grad_quarter, query_grad)


def solution(mesh):
    seq, exp, head = mesh.shape["seq"], mesh.shape["exp"], mesh.shape["head"]
    fine = Mesh(mesh.devices.reshape(seq // 2, 2, exp, head), ("z", "core", "exp", "head"))
    seq_axes = ("z", "core")
    in_specs = (
        P(seq_axes, None),
        P(seq_axes, None),
        P(),
        P(seq_axes, None),
        P(seq_axes, None),
        P("exp", None, seq_axes),
        P("exp", None, seq_axes),
        P("exp", seq_axes, None),
        P(("exp", "head"), None),
        P(seq_axes, ("exp", "head")),
        P(seq_axes, ("exp", "head")),
        P(seq_axes, ("exp", "head")),
    )
    out_specs = (P(("z", "core", "head"), None), P(seq_axes, ("exp", "head")))
    return jax.shard_map(
        per_device, mesh=fine, in_specs=in_specs, out_specs=out_specs, check_vma=False
    )
```

```python
import functools

import jax
import jax.numpy as jnp
from jax import lax
from jax.experimental import pallas as pl
from jax.experimental.pallas import tpu as pltpu
from jax.sharding import Mesh, PartitionSpec as P

HD = 128
EPSILON = 1e-05
CAP = 12
FOLD = 4
ROOM = 16
UNITS = 256
MIB = 2**20

CONTRACT = (((1,), (1,)), ((), ()))


def across(left, right):
    return lax.dot_general(left, right, CONTRACT, preferred_element_type=jnp.float32)


def two_terms(full):
    high = full.astype(jnp.bfloat16)
    return high, (full - high.astype(jnp.float32)).astype(jnp.bfloat16)


def expert_kernel(rows_hbm, own_hbm, other_hbm, out_ref, rows_ref, w_ref, back_ref, sems):
    shards, _, width = rows_ref.shape
    part = width // FOLD
    arrive = pltpu.make_async_copy(rows_hbm, rows_ref, sems.at[0])
    fetch = [
        [pltpu.make_async_copy(hbm.at[k], w_ref.at[c, k], sems.at[1 + 3 * c + k]) for k in range(3)]
        for c, hbm in enumerate((own_hbm, other_hbm))
    ]
    arrive.start()
    for copy in fetch[0] + fetch[1]:
        copy.start()
    arrive.wait()
    for c in range(2):
        ins = rows_ref[:, :ROOM, :].reshape(shards * ROOM, width)
        fetch[c][0].wait()
        gate_val = across(ins, w_ref[c, 0])
        fetch[c][1].wait()
        up_val = across(ins, w_ref[c, 1])
        fetch[c][2].wait()
        grads = rows_ref[:, ROOM:, :].reshape(shards * ROOM, width)
        hidden_grad = across(grads, w_ref[c, 2])
        sigma = jax.nn.sigmoid(gate_val)
        gate_grad = (hidden_grad * up_val * sigma * (1.0 + gate_val * (1.0 - sigma))).astype(
            jnp.bfloat16
        )
        up_grad = (hidden_grad * gate_val * sigma).astype(jnp.bfloat16)
        for q in range(FOLD):
            at = slice(q * part, (q + 1) * part)
            piece = jnp.dot(gate_grad, w_ref[c, 0, :, at], preferred_element_type=jnp.float32)
            piece = piece + jnp.dot(up_grad, w_ref[c, 1, :, at], preferred_element_type=jnp.float32)
            if c == 0:
                back_ref[q] = piece
            else:
                back_ref[q] += piece
    for shard in range(shards):
        at = slice(shard * ROOM, shard * ROOM + CAP)
        block = jnp.concatenate([back_ref[q, at, :] for q in range(FOLD)], axis=0)
        out_ref[shard] = block.astype(jnp.bfloat16)


def expert_block(rows, own, other):
    shards, depth, width = rows.shape
    out = (shards, FOLD * CAP, width // FOLD)
    return pl.pallas_call(
        expert_kernel,
        in_specs=[pl.BlockSpec(memory_space=pl.ANY)] * 3,
        out_specs=pl.BlockSpec(memory_space=pltpu.VMEM),
        out_shape=jax.ShapeDtypeStruct(out, jnp.bfloat16),
        scratch_shapes=[
            pltpu.VMEM(rows.shape, jnp.bfloat16),
            pltpu.VMEM((2, *own.shape), jnp.bfloat16),
            pltpu.VMEM((FOLD, shards * ROOM, width // FOLD), jnp.float32),
            pltpu.SemaphoreType.DMA((7,)),
        ],
        compiler_params=pltpu.CompilerParams(vmem_limit_bytes=58 * MIB),
        cost_estimate=pl.CostEstimate(
            flops=2 * 5 * shards * ROOM * 2 * UNITS * width,
            bytes_accessed=4 * own.size + 2 * rows.size,
            transcendentals=0,
        ),
        name="expert_block",
    )(rows, own, other)


def sum_kernel(in_ref, out_ref):
    total = jnp.sum(in_ref[...].astype(jnp.float32), axis=0).astype(jnp.bfloat16)
    for copy in range(out_ref.shape[0]):
        out_ref[copy] = total


def rows_kernel(
    head_ref,
    slots_ref,
    picks_ref,
    fold_ref,
    resid_ref,
    grad_ref,
    gain_ref,
    *rest,
):
    *w_hbm, back_ref, part_ref, w_ref, sems = rest
    fetch = [pltpu.make_async_copy(w, w_ref.at[d], sems.at[d]) for d, w in enumerate(w_hbm)]
    for copy in fetch:
        copy.start()
    flat = slots_ref[...].reshape(-1, slots_ref.shape[2])
    fold = fold_ref[...]
    picks = picks_ref[...]
    pieces = [
        jnp.dot(
            jnp.where(fold == q, picks, 0.0).astype(jnp.bfloat16),
            flat,
            preferred_element_type=jnp.float32,
        )
        for q in range(FOLD)
    ]
    summed = jnp.concatenate(pieces, axis=1)
    resid_full = resid_ref[...].astype(jnp.float32)
    inv_rms = lax.rsqrt(jnp.mean(resid_full * resid_full, axis=-1, keepdims=True) + EPSILON)
    grad_full = grad_ref[...].astype(jnp.float32)
    back = norm_back(resid_full, inv_rms, grad_full, gain_ref[...], summed)
    back_ref[...] = back
    for d, copy in enumerate(fetch):
        copy.wait()
        there = lax.rem(head_ref[0] + d, len(fetch))
        part_ref[there] = across(back, w_ref[d]).astype(jnp.bfloat16)


def early_kernel(scale, query_ref, key_ref, value_ref, qpos_ref, kpos_ref, prob_ref, out_ref):
    allowed = kpos_ref[...] <= qpos_ref[...]
    scores = jnp.where(allowed, across(query_ref[...], key_ref[...]) * scale, -1e30)
    row_max = jnp.max(scores, axis=-1, keepdims=True)
    expo_vals = jnp.where(allowed, jnp.exp(scores - row_max), 0.0)
    probs = expo_vals / jnp.sum(expo_vals, axis=-1, keepdims=True)
    prob_ref[...] = probs
    high, low = two_terms(probs)
    values = value_ref[...]
    out_ref[...] = jnp.dot(high, values, preferred_element_type=jnp.float32) + jnp.dot(
        low, values, preferred_element_type=jnp.float32
    )


def late_kernel(scale, grad_ref, key_ref, value_ref, prob_ref, out_ref, back_ref):
    grads = grad_ref[...]
    delta = jnp.sum(grads.astype(jnp.float32) * out_ref[...], axis=-1, keepdims=True)
    mixed = prob_ref[...] * (across(grads, value_ref[...]) - delta)
    high, low = two_terms(mixed)
    keys = key_ref[...]
    total = jnp.dot(high, keys, preferred_element_type=jnp.float32) + jnp.dot(
        low, keys, preferred_element_type=jnp.float32
    )
    back_ref[...] = (scale * total).astype(jnp.bfloat16)


def in_vmem(kernel, out_shape, name, flops, *args, fetched=(), scratch=(), limit=32):
    places = [pltpu.SMEM if a.size == 1 else pltpu.VMEM for a in args]
    places = places + [pl.ANY] * len(fetched)
    return pl.pallas_call(
        kernel,
        in_specs=[pl.BlockSpec(memory_space=place) for place in places],
        out_specs=jax.tree.map(lambda _: pl.BlockSpec(memory_space=pltpu.VMEM), out_shape),
        out_shape=out_shape,
        compiler_params=pltpu.CompilerParams(vmem_limit_bytes=limit * MIB),
        cost_estimate=pl.CostEstimate(flops=flops, bytes_accessed=4 * MIB, transcendentals=0),
        scratch_shapes=list(scratch),
        name=name,
    )(*args, *fetched)


def core_swap(block):
    return lax.ppermute(block, "core", [(0, 1), (1, 0)])


def norm_back(resid_full, inv_rms, grad_rows, norm_gain, expert_grad):
    scaled_grad = norm_gain.astype(jnp.float32) * expert_grad
    cubed = inv_rms * inv_rms * inv_rms
    mean_term = jnp.mean(scaled_grad * resid_full, axis=-1, keepdims=True)
    return (grad_rows + inv_rms * scaled_grad - resid_full * cubed * mean_term).astype(jnp.bfloat16)


def per_device(
    resid,
    grad_out,
    norm_gain,
    expert_ids,
    route_weights,
    w_gate,
    w_up,
    w_down,
    w_out,
    queries,
    keys,
    values,
):
    f32, bf16 = jnp.float32, jnp.bfloat16
    tok_rows, width = resid.shape
    z_count, exp_count, head_count = (lax.axis_size(a) for a in ("z", "exp", "head"))
    z_index, core_index = lax.axis_index("z"), lax.axis_index("core")
    exp_index, head_index = lax.axis_index("exp"), lax.axis_index("head")
    quarter = tok_rows // head_count
    row_first = head_index * quarter
    resid_part = lax.dynamic_slice_in_dim(resid, row_first, quarter, 0)
    grad_part = lax.dynamic_slice_in_dim(grad_out, row_first, quarter, 0)
    ids_part = lax.dynamic_slice_in_dim(expert_ids, row_first, quarter, 0)
    weights_part = lax.dynamic_slice_in_dim(route_weights, row_first, quarter, 0)
    resid_full = resid_part.astype(f32)
    inv_rms = lax.rsqrt(jnp.mean(resid_full * resid_full, axis=-1, keepdims=True) + EPSILON)
    normed = (resid_full * inv_rms * norm_gain.astype(f32)).astype(bf16)
    grad_full = grad_part.astype(f32)

    row_ids = jnp.arange(quarter, dtype=jnp.int32)
    earlier = row_ids[:, None] < row_ids[None, :]

    def slots_of(expert):
        matched = ids_part == expert
        routed = jnp.any(matched, axis=1)
        position = jnp.sum((earlier & routed[:, None]).astype(jnp.int32), axis=0)
        weight = jnp.sum(jnp.where(matched, weights_part, 0.0), axis=1)
        return routed, position, weight

    routed, position, weight = slots_of(exp_index)
    slot_ids = jnp.arange(ROOM, dtype=jnp.int32)
    select = ((position[None, :] == slot_ids[:CAP, None]) & routed[None, :]).astype(bf16)
    scaled = (weight[:, None] * grad_full).astype(bf16)
    slot_in = jnp.dot(select, normed, preferred_element_type=f32).astype(bf16)
    slot_grad = jnp.dot(select, scaled, preferred_element_type=f32).astype(bf16)
    spare = ROOM - CAP
    mine = jnp.concatenate(
        [slot_in, keys.reshape(spare, -1), slot_grad, values.reshape(spare, -1)], axis=0
    )

    rows = lax.all_gather(mine, "z", axis=0, tiled=True).reshape(z_count, 2 * ROOM, width)
    gate_mat, up_mat, down_mat, w_mine, mine = lax.optimization_barrier(
        (w_gate[0].T, w_up[0].T, w_down[0], w_out, mine)
    )
    fill = ((0, UNITS - gate_mat.shape[0]), (0, 0))
    own = jnp.stack([jnp.pad(w, fill) for w in (gate_mat, up_mat, down_mat)], axis=0)
    other = core_swap(own)
    w_near = [w_mine] + [
        lax.ppermute(w_mine, "head", [(a, (a - d) % head_count) for a in range(head_count)])
        for d in range(1, head_count)
    ]
    other, *w_near = lax.optimization_barrier((other, *w_near))

    packed = rows.reshape(z_count, 2, ROOM, width)[:, :, CAP:]
    packed = jnp.stack([packed, core_swap(packed)], axis=0)
    key_all = packed[:, :, 0].reshape(-1, HD)
    value_all = packed[:, :, 1].reshape(-1, HD)
    query_pos = (z_index * 2 + core_index) * tok_rows + jnp.arange(tok_rows, dtype=jnp.int32)
    place = jnp.arange(2 * z_count * tok_rows, dtype=jnp.int32)
    half = z_count * tok_rows
    shard = (place % half) // tok_rows * 2 + (core_index + place // half) % 2
    key_pos = shard * tok_rows + place % tok_rows
    scale = HD ** (-0.5)
    attn_flops = 2 * tok_rows * HD * 2 * half
    probs, output = in_vmem(
        functools.partial(early_kernel, scale),
        [
            jax.ShapeDtypeStruct((tok_rows, 2 * half), f32),
            jax.ShapeDtypeStruct((tok_rows, HD), f32),
        ],
        "attention_early",
        3 * attn_flops,
        queries,
        key_all,
        value_all,
        query_pos[:, None],
        key_pos[None, :],
    )

    leave = expert_block(rows, own, other)
    came = lax.all_to_all(leave, "z", 0, 0, tiled=True)
    came, probs, output, key_all, value_all = lax.optimization_barrier(
        (came, probs, output, key_all, value_all)
    )
    slots = in_vmem(
        sum_kernel,
        jax.ShapeDtypeStruct((exp_count, *came.shape[1:]), bf16),
        "slot_sum",
        came.size,
        came,
    )
    slots = lax.all_to_all(slots, "exp", 0, 0, tiled=True)
    picks = []
    for expert in range(exp_count):
        routed, position, _ = slots_of(expert)
        picks.append((position[:, None] == slot_ids[None, :CAP]) & routed[:, None])
    picks = jnp.stack(picks, axis=1).astype(f32)[:, :, None, :]
    picks = jnp.broadcast_to(picks, (quarter, exp_count, FOLD, CAP)).reshape(quarter, -1)
    fold = jnp.arange(picks.shape[1], dtype=jnp.int32) // CAP % FOLD
    grad_quarter, at_heads = in_vmem(
        rows_kernel,
        [
            jax.ShapeDtypeStruct((quarter, width), bf16),
            jax.ShapeDtypeStruct((head_count, quarter, HD), bf16),
        ],
        "token_rows",
        2 * quarter * width * (picks.shape[1] + head_count * HD),
        head_index.reshape(1),
        slots,
        picks,
        fold[None, :],
        resid_part,
        grad_part,
        norm_gain[None, :],
        fetched=w_near,
        limit=58,
        scratch=(
            pltpu.VMEM((head_count, *w_out.shape), bf16),
            pltpu.SemaphoreType.DMA((head_count,)),
        ),
    )
    attn_grad = lax.all_to_all(at_heads, "head", 0, 0, tiled=True).reshape(tok_rows, HD)
    query_grad = in_vmem(
        functools.partial(late_kernel, scale),
        jax.ShapeDtypeStruct((tok_rows, HD), bf16),
        "attention_late",
        3 * attn_flops,
        attn_grad,
        key_all,
        value_all,
        probs,
        output,
    )
    return (grad_quarter, query_grad)


def solution(mesh):
    seq, exp, head = mesh.shape["seq"], mesh.shape["exp"], mesh.shape["head"]
    fine = Mesh(mesh.devices.reshape(seq // 2, 2, exp, head), ("z", "core", "exp", "head"))
    seq_axes = ("z", "core")
    in_specs = (
        P(seq_axes, None),
        P(seq_axes, None),
        P(),
        P(seq_axes, None),
        P(seq_axes, None),
        P("exp", None, seq_axes),
        P("exp", None, seq_axes),
        P("exp", seq_axes, None),
        P(("exp", "head"), None),
        P(seq_axes, ("exp", "head")),
        P(seq_axes, ("exp", "head")),
        P(seq_axes, ("exp", "head")),
    )
    out_specs = (P(("z", "core", "head"), None), P(seq_axes, ("exp", "head")))
    return jax.shard_map(
        per_device, mesh=fine, in_specs=in_specs, out_specs=out_specs, check_vma=False
    )
```

```python
import functools

import jax
import jax.numpy as jnp
from jax import lax
from jax.experimental import pallas as pl
from jax.experimental.pallas import tpu as pltpu
from jax.sharding import Mesh, PartitionSpec as P

HD = 128
EPSILON = 1e-05
CAP = 12
FOLD = 4
ROOM = 16
UNITS = 256
MIB = 2**20

CONTRACT = (((1,), (1,)), ((), ()))


def across(left, right):
    return lax.dot_general(left, right, CONTRACT, preferred_element_type=jnp.float32)


def two_terms(full):
    high = full.astype(jnp.bfloat16)
    return high, (full - high.astype(jnp.float32)).astype(jnp.bfloat16)


def expert_kernel(
    order_ref, rows_hbm, own_hbm, other_hbm, stay_ref, leave_ref, rows_ref, w_ref, back_ref, sems
):
    shards, _, width = rows_ref.shape
    part = width // FOLD
    arrive = pltpu.make_async_copy(rows_hbm, rows_ref, sems.at[0])
    fetch = [
        [pltpu.make_async_copy(hbm.at[k], w_ref.at[c, k], sems.at[1 + 3 * c + k]) for k in range(3)]
        for c, hbm in enumerate((own_hbm, other_hbm))
    ]
    coming = [arrive] + fetch[0] + fetch[1]
    for copy in coming[:3]:
        copy.start()

    def take(index):
        coming[index].wait()
        if index + 3 < len(coming):
            coming[index + 3].start()

    take(0)
    for c in range(2):
        ins = rows_ref[:, :ROOM, :].reshape(shards * ROOM, width)
        take(3 * c + 1)
        gate_val = across(ins, w_ref[c, 0])
        take(3 * c + 2)
        up_val = across(ins, w_ref[c, 1])
        take(3 * c + 3)
        grads = rows_ref[:, ROOM:, :].reshape(shards * ROOM, width)
        hidden_grad = across(grads, w_ref[c, 2])
        sigma = jax.nn.sigmoid(gate_val)
        gate_grad = (hidden_grad * up_val * sigma * (1.0 + gate_val * (1.0 - sigma))).astype(
            jnp.bfloat16
        )
        up_grad = (hidden_grad * gate_val * sigma).astype(jnp.bfloat16)
        for q in range(FOLD):
            at = slice(q * part, (q + 1) * part)
            piece = jnp.dot(gate_grad, w_ref[c, 0, :, at], preferred_element_type=jnp.float32)
            piece = piece + jnp.dot(up_grad, w_ref[c, 1, :, at], preferred_element_type=jnp.float32)
            if c == 0:
                back_ref[q] = piece
            else:
                back_ref[q] += piece
    for k in range(shards):
        at = pl.ds(pl.multiple_of(order_ref[k] * ROOM, ROOM), CAP)
        block = jnp.concatenate([back_ref[q, at, :] for q in range(FOLD)], axis=0)
        out_ref = stay_ref if k < shards // 2 else leave_ref
        out_ref[k % (shards // 2)] = block.astype(jnp.bfloat16)


def expert_block(order, rows, own, other):
    shards, depth, width = rows.shape
    out = (shards // 2, FOLD * CAP, width // FOLD)
    return pl.pallas_call(
        expert_kernel,
        in_specs=[pl.BlockSpec(memory_space=pltpu.SMEM)] + [pl.BlockSpec(memory_space=pl.ANY)] * 3,
        out_specs=[pl.BlockSpec(memory_space=pltpu.VMEM)] * 2,
        out_shape=[jax.ShapeDtypeStruct(out, jnp.bfloat16)] * 2,
        scratch_shapes=[
            pltpu.VMEM(rows.shape, jnp.bfloat16),
            pltpu.VMEM((2, *own.shape), jnp.bfloat16),
            pltpu.VMEM((FOLD, shards * ROOM, width // FOLD), jnp.float32),
            pltpu.SemaphoreType.DMA((7,)),
        ],
        compiler_params=pltpu.CompilerParams(vmem_limit_bytes=58 * MIB),
        cost_estimate=pl.CostEstimate(
            flops=2 * 5 * shards * ROOM * 2 * UNITS * width,
            bytes_accessed=4 * own.size + 2 * rows.size,
            transcendentals=0,
        ),
        name="expert_block",
    )(order, rows, own, other)


def sum_kernel(in_ref, out_ref):
    total = jnp.sum(in_ref[...].astype(jnp.float32), axis=0).astype(jnp.bfloat16)
    for copy in range(out_ref.shape[0]):
        out_ref[copy] = total


def rows_kernel(
    head_ref,
    slots_ref,
    picks_ref,
    fold_ref,
    resid_ref,
    grad_ref,
    gain_ref,
    *rest,
):
    *w_hbm, back_ref, part_ref, w_ref, sems = rest
    fetch = [pltpu.make_async_copy(w, w_ref.at[d], sems.at[d]) for d, w in enumerate(w_hbm)]
    for copy in fetch:
        copy.start()
    flat = slots_ref[...].reshape(-1, slots_ref.shape[2])
    fold = fold_ref[...]
    picks = picks_ref[...].T
    pieces = [
        jnp.dot(
            jnp.where(fold == q, picks, 0.0).astype(jnp.bfloat16),
            flat,
            preferred_element_type=jnp.float32,
        )
        for q in range(FOLD)
    ]
    summed = jnp.concatenate(pieces, axis=1)
    resid_full = resid_ref[...].astype(jnp.float32)
    inv_rms = lax.rsqrt(jnp.mean(resid_full * resid_full, axis=-1, keepdims=True) + EPSILON)
    grad_full = grad_ref[...].astype(jnp.float32)
    back = norm_back(resid_full, inv_rms, grad_full, gain_ref[...], summed)
    back_ref[...] = back
    for d, copy in enumerate(fetch):
        copy.wait()
        there = lax.rem(head_ref[0] + d, len(fetch))
        part_ref[there] = across(w_ref[d], back).T.astype(jnp.bfloat16)


def early_kernel(scale, query_ref, key0, key1, value0, value1, qpos_ref, kpos_ref, prob_ref, out_ref):
    allowed = kpos_ref[...] <= qpos_ref[...]
    keys = jnp.concatenate([key0[...], key1[...]], axis=0)
    scores = jnp.where(allowed, across(query_ref[...], keys) * scale, -1e30)
    row_max = jnp.max(scores, axis=-1, keepdims=True)
    expo_vals = jnp.where(allowed, jnp.exp(scores - row_max), 0.0)
    probs = expo_vals / jnp.sum(expo_vals, axis=-1, keepdims=True)
    prob_ref[...] = probs
    high, low = two_terms(probs)
    values = jnp.concatenate([value0[...], value1[...]], axis=0)
    out_ref[...] = jnp.dot(high, values, preferred_element_type=jnp.float32) + jnp.dot(
        low, values, preferred_element_type=jnp.float32
    )


def late_kernel(scale, grad_ref, key0, key1, value0, value1, prob_ref, out_ref, back_ref):
    grads = grad_ref[...]
    delta = jnp.sum(grads.astype(jnp.float32) * out_ref[...], axis=-1, keepdims=True)
    values = jnp.concatenate([value0[...], value1[...]], axis=0)
    mixed = prob_ref[...] * (across(grads, values) - delta)
    high, low = two_terms(mixed)
    keys = jnp.concatenate([key0[...], key1[...]], axis=0)
    total = jnp.dot(high, keys, preferred_element_type=jnp.float32) + jnp.dot(
        low, keys, preferred_element_type=jnp.float32
    )
    back_ref[...] = (scale * total).astype(jnp.bfloat16)


def in_vmem(kernel, out_shape, name, flops, *args, fetched=(), scratch=(), limit=32):
    places = [pltpu.SMEM if a.size == 1 else pltpu.VMEM for a in args]
    places = places + [pl.ANY] * len(fetched)
    return pl.pallas_call(
        kernel,
        in_specs=[pl.BlockSpec(memory_space=place) for place in places],
        out_specs=jax.tree.map(lambda _: pl.BlockSpec(memory_space=pltpu.VMEM), out_shape),
        out_shape=out_shape,
        compiler_params=pltpu.CompilerParams(vmem_limit_bytes=limit * MIB),
        cost_estimate=pl.CostEstimate(flops=flops, bytes_accessed=4 * MIB, transcendentals=0),
        scratch_shapes=list(scratch),
        name=name,
    )(*args, *fetched)


def core_swap(block):
    return lax.ppermute(block, "core", [(0, 1), (1, 0)])


def norm_back(resid_full, inv_rms, grad_rows, norm_gain, expert_grad):
    scaled_grad = norm_gain.astype(jnp.float32) * expert_grad
    cubed = inv_rms * inv_rms * inv_rms
    mean_term = jnp.mean(scaled_grad * resid_full, axis=-1, keepdims=True)
    return (grad_rows + inv_rms * scaled_grad - resid_full * cubed * mean_term).astype(jnp.bfloat16)


def per_device(
    resid,
    grad_out,
    norm_gain,
    expert_ids,
    route_weights,
    w_gate,
    w_up,
    w_down,
    w_out,
    queries,
    keys,
    values,
):
    f32, bf16 = jnp.float32, jnp.bfloat16
    tok_rows, width = resid.shape
    z_count, exp_count, head_count = (lax.axis_size(a) for a in ("z", "exp", "head"))
    z_index, core_index = lax.axis_index("z"), lax.axis_index("core")
    exp_index, head_index = lax.axis_index("exp"), lax.axis_index("head")
    quarter = tok_rows // head_count
    row_first = head_index * quarter
    resid_part = lax.dynamic_slice_in_dim(resid, row_first, quarter, 0)
    grad_part = lax.dynamic_slice_in_dim(grad_out, row_first, quarter, 0)
    ids_part = lax.dynamic_slice_in_dim(expert_ids, row_first, quarter, 0)
    weights_part = lax.dynamic_slice_in_dim(route_weights, row_first, quarter, 0)
    resid_full = resid_part.astype(f32)
    inv_rms = lax.rsqrt(jnp.mean(resid_full * resid_full, axis=-1, keepdims=True) + EPSILON)
    normed = (resid_full * inv_rms * norm_gain.astype(f32)).astype(bf16)
    grad_full = grad_part.astype(f32)

    row_ids = jnp.arange(quarter, dtype=jnp.int32)
    earlier = row_ids[:, None] < row_ids[None, :]

    def slots_of(expert):
        matched = ids_part == expert
        routed = jnp.any(matched, axis=1)
        position = jnp.sum((earlier & routed[:, None]).astype(jnp.int32), axis=0)
        weight = jnp.sum(jnp.where(matched, weights_part, 0.0), axis=1)
        return routed, position, weight

    routed, position, weight = slots_of(exp_index)
    slot_ids = jnp.arange(ROOM, dtype=jnp.int32)
    select = ((position[None, :] == slot_ids[:CAP, None]) & routed[None, :]).astype(bf16)
    scaled = (weight[:, None] * grad_full).astype(bf16)
    slot_in = jnp.dot(select, normed, preferred_element_type=f32).astype(bf16)
    slot_grad = jnp.dot(select, scaled, preferred_element_type=f32).astype(bf16)
    spare = ROOM - CAP
    mine = jnp.concatenate(
        [slot_in, keys.reshape(spare, -1), slot_grad, values.reshape(spare, -1)], axis=0
    )

    rows = lax.all_gather(mine, "z", axis=0, tiled=True).reshape(z_count, 2 * ROOM, width)
    gate_mat, up_mat, down_mat, w_mine, mine = lax.optimization_barrier(
        (w_gate[0].T, w_up[0].T, w_down[0], w_out, mine)
    )
    fill = ((0, UNITS - gate_mat.shape[0]), (0, 0))
    own = jnp.stack([jnp.pad(w, fill) for w in (gate_mat, up_mat, down_mat)], axis=0)
    other = core_swap(own)
    w_near = [w_mine] + [
        lax.ppermute(w_mine, "head", [(a, (a - d) % head_count) for a in range(head_count)])
        for d in range(1, head_count)
    ]
    picks = []
    for expert in range(exp_count):
        routed, position, _ = slots_of(expert)
        picks.append((position[:, None] == slot_ids[None, :CAP]) & routed[:, None])
    picks = jnp.stack(picks, axis=1).astype(f32)[:, :, None, :]
    picks = jnp.broadcast_to(picks, (quarter, exp_count, FOLD, CAP)).reshape(quarter, -1).T
    fold = jnp.arange(picks.shape[0], dtype=jnp.int32) // CAP % FOLD
    fold, gain_row = fold[None, :], norm_gain[None, :]
    other, picks, fold, gain_row, resid_part, grad_part, *w_near = lax.optimization_barrier(
        (other, picks, fold, gain_row, resid_part, grad_part, *w_near)
    )

    toward = 1 - 2 * core_index
    fours = 4 * jnp.arange(z_count // 4, dtype=jnp.int32)
    next_index = z_index + toward + z_count
    order = jnp.concatenate(
        [fours + p % 4 for p in (z_index, z_index + 2, next_index, next_index + 2)]
    )
    stay, leave = expert_block(order, rows, own, other)

    leave, rows = lax.optimization_barrier((leave, rows))
    packed = rows.reshape(z_count, 2, ROOM, width)[:, :, CAP:]
    both = (packed, core_swap(packed))
    key_all = [block[:, 0].reshape(-1, HD) for block in both]
    value_all = [block[:, 1].reshape(-1, HD) for block in both]
    query_pos = (z_index * 2 + core_index) * tok_rows + jnp.arange(tok_rows, dtype=jnp.int32)
    place = jnp.arange(2 * z_count * tok_rows, dtype=jnp.int32)
    half = z_count * tok_rows
    shard = (place % half) // tok_rows * 2 + (core_index + place // half) % 2
    key_pos = shard * tok_rows + place % tok_rows
    scale = HD ** (-0.5)
    attn_flops = 2 * tok_rows * HD * 2 * half
    probs, output = in_vmem(
        functools.partial(early_kernel, scale),
        [
            jax.ShapeDtypeStruct((tok_rows, 2 * half), f32),
            jax.ShapeDtypeStruct((tok_rows, HD), f32),
        ],
        "attention_early",
        3 * attn_flops,
        queries,
        *key_all,
        *value_all,
        query_pos[:, None],
        key_pos[None, :],
    )

    def step(block, dist):
        up = [(2 * a, 2 * ((a + dist) % z_count)) for a in range(z_count)]
        down = [(2 * a + 1, 2 * ((a - dist) % z_count) + 1) for a in range(z_count)]
        return lax.ppermute(block, ("z", "core"), up + down)

    few = z_count // 4
    came = step(leave, 1)
    far = (stay[few:].astype(f32) + came[few:].astype(f32)).astype(bf16)
    came_far = step(far, 2)
    near = stay[:few].astype(f32) + came[:few].astype(f32) + came_far.astype(f32)
    near, probs, output, key_all, value_all = lax.optimization_barrier(
        (near.astype(bf16), probs, output, key_all, value_all)
    )
    same = [list(range(r, z_count, 4)) for r in range(4)]
    came = lax.all_to_all(near, "z", 0, 0, tiled=True, axis_index_groups=same)
    slots = in_vmem(
        sum_kernel,
        jax.ShapeDtypeStruct((exp_count, *came.shape[1:]), bf16),
        "slot_sum",
        came.size,
        came,
    )
    slots = lax.all_to_all(slots, "exp", 0, 0, tiled=True)
    grad_quarter, at_heads = in_vmem(
        rows_kernel,
        [
            jax.ShapeDtypeStruct((quarter, width), bf16),
            jax.ShapeDtypeStruct((head_count, quarter, HD), bf16),
        ],
        "token_rows",
        2 * quarter * width * (picks.shape[0] + head_count * HD),
        head_index.reshape(1),
        slots,
        picks,
        fold,
        resid_part,
        grad_part,
        gain_row,
        fetched=w_near,
        limit=58,
        scratch=(
            pltpu.VMEM((head_count, *w_out.shape), bf16),
            pltpu.SemaphoreType.DMA((head_count,)),
        ),
    )
    attn_grad = lax.all_to_all(at_heads, "head", 0, 0, tiled=True).reshape(tok_rows, HD)
    query_grad = in_vmem(
        functools.partial(late_kernel, scale),
        jax.ShapeDtypeStruct((tok_rows, HD), bf16),
        "attention_late",
        3 * attn_flops,
        attn_grad,
        *key_all,
        *value_all,
        probs,
        output,
    )
    return (grad_quarter, query_grad)


def solution(mesh):
    seq, exp, head = mesh.shape["seq"], mesh.shape["exp"], mesh.shape["head"]
    fine = Mesh(mesh.devices.reshape(seq // 2, 2, exp, head), ("z", "core", "exp", "head"))
    seq_axes = ("z", "core")
    in_specs = (
        P(seq_axes, None),
        P(seq_axes, None),
        P(),
        P(seq_axes, None),
        P(seq_axes, None),
        P("exp", None, seq_axes),
        P("exp", None, seq_axes),
        P("exp", seq_axes, None),
        P(("exp", "head"), None),
        P(seq_axes, ("exp", "head")),
        P(seq_axes, ("exp", "head")),
        P(seq_axes, ("exp", "head")),
    )
    out_specs = (P(("z", "core", "head"), None), P(seq_axes, ("exp", "head")))
    return jax.shard_map(
        per_device, mesh=fine, in_specs=in_specs, out_specs=out_specs, check_vma=False
    )
```

```python
import functools

import jax
import jax.numpy as jnp
from jax import lax
from jax.experimental import pallas as pl
from jax.experimental.pallas import tpu as pltpu
from jax.sharding import Mesh, PartitionSpec as P

HD = 128
EPSILON = 1e-05
CAP = 12
FOLD = 4
ROOM = 16
UNITS = 256
MIB = 2**20

CONTRACT = (((1,), (1,)), ((), ()))


def across(left, right):
    return lax.dot_general(left, right, CONTRACT, preferred_element_type=jnp.float32)


def two_terms(full):
    high = full.astype(jnp.bfloat16)
    return high, (full - high.astype(jnp.float32)).astype(jnp.bfloat16)


def expert_kernel(bit_ref, rows_ref, w_ref, stay_ref, leave_ref, back_ref):
    step = pl.program_id(0)
    shards, _, width = rows_ref.shape
    part = width // FOLD
    ins = rows_ref[:, :ROOM, :].reshape(shards * ROOM, width)
    grads = rows_ref[:, ROOM:, :].reshape(shards * ROOM, width)
    gate_val = across(ins, w_ref[0, 0])
    up_val = across(ins, w_ref[0, 1])
    hidden_grad = across(grads, w_ref[0, 2])
    sigma = jax.nn.sigmoid(gate_val)
    gate_grad = (hidden_grad * up_val * sigma * (1.0 + gate_val * (1.0 - sigma))).astype(jnp.bfloat16)
    up_grad = (hidden_grad * gate_val * sigma).astype(jnp.bfloat16)
    for q in range(FOLD):
        at = slice(q * part, (q + 1) * part)
        piece = jnp.dot(gate_grad, w_ref[0, 0, :, at], preferred_element_type=jnp.float32)
        piece = piece + jnp.dot(up_grad, w_ref[0, 1, :, at], preferred_element_type=jnp.float32)
        piece = piece.reshape(shards, ROOM, part)

        @pl.when(step == 0)
        def _():
            back_ref[:, :, at] = piece

        @pl.when(step == 1)
        def _():
            back_ref[:, :, at] += piece

    @pl.when(step == 1)
    def _():
        bit = bit_ref[0]

        def folded(shard):
            block = back_ref[shard]
            return jnp.concatenate([block[:CAP, q * part : (q + 1) * part] for q in range(FOLD)], axis=0)

        for k in range(shards // 2):
            stay_ref[k] = folded(2 * k + bit)
            leave_ref[k] = folded(2 * k + 1 - bit).astype(jnp.bfloat16)


def expert_block(bit, rows, weights):
    shards, depth, width = rows.shape
    out = (shards // 2, FOLD * CAP, width // FOLD)
    return pl.pallas_call(
        expert_kernel,
        grid=(2,),
        in_specs=[
            pl.BlockSpec(memory_space=pltpu.SMEM),
            pl.BlockSpec((shards, depth, width), lambda i: (0, 0, 0)),
            pl.BlockSpec((1, 3, UNITS, width), lambda i: (i, 0, 0, 0)),
        ],
        out_specs=[pl.BlockSpec(out, lambda i: (0, 0, 0))] * 2,
        out_shape=[
            jax.ShapeDtypeStruct(out, jnp.float32),
            jax.ShapeDtypeStruct(out, jnp.bfloat16),
        ],
        scratch_shapes=[pltpu.VMEM((shards, ROOM, width), jnp.float32)],
        compiler_params=pltpu.CompilerParams(vmem_limit_bytes=48 * MIB),
        cost_estimate=pl.CostEstimate(
            flops=2 * 5 * shards * ROOM * 2 * UNITS * width,
            bytes_accessed=2 * weights.size + 2 * rows.size,
            transcendentals=0,
        ),
        name="expert_block",
    )(bit, rows, weights)


def early_kernel(scale, query_ref, key_ref, value_ref, qpos_ref, kpos_ref, prob_ref, out_ref):
    allowed = kpos_ref[...] <= qpos_ref[...]
    scores = jnp.where(allowed, across(query_ref[...], key_ref[...]) * scale, -1e30)
    row_max = jnp.max(scores, axis=-1, keepdims=True)
    expo_vals = jnp.where(allowed, jnp.exp(scores - row_max), 0.0)
    probs = expo_vals / jnp.sum(expo_vals, axis=-1, keepdims=True)
    prob_ref[...] = probs
    high, low = two_terms(probs)
    values = value_ref[...]
    out_ref[...] = jnp.dot(high, values, preferred_element_type=jnp.float32) + jnp.dot(
        low, values, preferred_element_type=jnp.float32
    )


def late_kernel(scale, grad_ref, key_ref, value_ref, prob_ref, out_ref, back_ref):
    grads = grad_ref[...]
    delta = jnp.sum(grads.astype(jnp.float32) * out_ref[...], axis=-1, keepdims=True)
    mixed = prob_ref[...] * (across(grads, value_ref[...]) - delta)
    high, low = two_terms(mixed)
    keys = key_ref[...]
    total = jnp.dot(high, keys, preferred_element_type=jnp.float32) + jnp.dot(
        low, keys, preferred_element_type=jnp.float32
    )
    back_ref[...] = (scale * total).astype(jnp.bfloat16)


def in_vmem(kernel, out_shape, name, flops, *args):
    return pl.pallas_call(
        kernel,
        in_specs=[pl.BlockSpec(memory_space=pltpu.VMEM)] * len(args),
        out_specs=jax.tree.map(lambda _: pl.BlockSpec(memory_space=pltpu.VMEM), out_shape),
        out_shape=out_shape,
        compiler_params=pltpu.CompilerParams(vmem_limit_bytes=32 * MIB),
        cost_estimate=pl.CostEstimate(flops=flops, bytes_accessed=4 * MIB, transcendentals=0),
        name=name,
    )(*args)


def core_swap(block):
    return lax.ppermute(block, "core", [(0, 1), (1, 0)])


def norm_back(resid_full, inv_rms, grad_rows, norm_gain, expert_grad):
    scaled_grad = norm_gain.astype(jnp.float32) * expert_grad
    cubed = inv_rms * inv_rms * inv_rms
    mean_term = jnp.mean(scaled_grad * resid_full, axis=-1, keepdims=True)
    return (grad_rows + inv_rms * scaled_grad - resid_full * cubed * mean_term).astype(jnp.bfloat16)


def per_device(
    resid,
    grad_out,
    norm_gain,
    expert_ids,
    route_weights,
    w_gate,
    w_up,
    w_down,
    w_out,
    queries,
    keys,
    values,
):
    f32, bf16 = jnp.float32, jnp.bfloat16
    tok_rows, width = resid.shape
    z_count, exp_count, head_count = (lax.axis_size(a) for a in ("z", "exp", "head"))
    z_index, core_index = lax.axis_index("z"), lax.axis_index("core")
    exp_index, head_index = lax.axis_index("exp"), lax.axis_index("head")
    quarter = tok_rows // head_count
    row_first = head_index * quarter
    resid_part = lax.dynamic_slice_in_dim(resid, row_first, quarter, 0)
    grad_part = lax.dynamic_slice_in_dim(grad_out, row_first, quarter, 0)
    ids_part = lax.dynamic_slice_in_dim(expert_ids, row_first, quarter, 0)
    weights_part = lax.dynamic_slice_in_dim(route_weights, row_first, quarter, 0)
    resid_full = resid_part.astype(f32)
    inv_rms = lax.rsqrt(jnp.mean(resid_full * resid_full, axis=-1, keepdims=True) + EPSILON)
    normed = (resid_full * inv_rms * norm_gain.astype(f32)).astype(bf16)
    grad_full = grad_part.astype(f32)

    row_ids = jnp.arange(quarter, dtype=jnp.int32)
    earlier = row_ids[:, None] < row_ids[None, :]

    def slots_of(expert):
        matched = ids_part == expert
        routed = jnp.any(matched, axis=1)
        position = jnp.sum((earlier & routed[:, None]).astype(jnp.int32), axis=0)
        weight = jnp.sum(jnp.where(matched, weights_part, 0.0), axis=1)
        return routed, position, weight

    routed, position, weight = slots_of(exp_index)
    slot_ids = jnp.arange(ROOM, dtype=jnp.int32)
    select = ((position[None, :] == slot_ids[:CAP, None]) & routed[None, :]).astype(bf16)
    scaled = (weight[:, None] * grad_full).astype(bf16)
    slot_in = jnp.dot(select, normed, preferred_element_type=f32).astype(bf16)
    slot_grad = jnp.dot(select, scaled, preferred_element_type=f32).astype(bf16)
    spare = ROOM - CAP
    mine = jnp.concatenate(
        [slot_in, keys.reshape(spare, -1), slot_grad, values.reshape(spare, -1)], axis=0
    )

    rows = lax.all_gather(mine, "z", axis=0, tiled=True).reshape(z_count, 2 * ROOM, width)
    gate_mat, up_mat, down_mat, w_mine, mine = lax.optimization_barrier(
        (w_gate[0].T, w_up[0].T, w_down[0], w_out, mine)
    )
    fill = ((0, UNITS - gate_mat.shape[0]), (0, 0))
    own = jnp.stack([jnp.pad(w, fill) for w in (gate_mat, up_mat, down_mat)], axis=0)
    weights = jnp.stack([own, core_swap(own)], axis=0)
    w_near = [w_mine] + [
        lax.ppermute(w_mine, "head", [(a, (a - d) % head_count) for a in range(head_count)])
        for d in range(1, head_count)
    ]
    w_four = jnp.concatenate(w_near, axis=0)
    picks = []
    for expert in range(exp_count):
        routed, position, _ = slots_of(expert)
        picks.append((position[:, None] == slot_ids[None, :CAP]) & routed[:, None])
    picks = jnp.stack(picks, axis=1).astype(bf16)
    theres = []
    for q in range(FOLD):
        there = jnp.zeros((quarter, exp_count, FOLD, CAP), bf16).at[:, :, q].set(picks)
        theres.append(there.reshape(quarter, -1))
    weights, w_four, *theres = lax.optimization_barrier((weights, w_four, *theres))

    packed = rows.reshape(z_count, 2, ROOM, width)[:, :, CAP:]
    packed = jnp.stack([packed, core_swap(packed)], axis=0)
    key_all = packed[:, :, 0].reshape(-1, HD)
    value_all = packed[:, :, 1].reshape(-1, HD)
    query_pos = (z_index * 2 + core_index) * tok_rows + jnp.arange(tok_rows, dtype=jnp.int32)
    place = jnp.arange(2 * z_count * tok_rows, dtype=jnp.int32)
    half = z_count * tok_rows
    shard = (place % half) // tok_rows * 2 + (core_index + place // half) % 2
    key_pos = shard * tok_rows + place % tok_rows
    scale = HD ** (-0.5)
    attn_flops = 2 * tok_rows * HD * 2 * half
    probs, output = in_vmem(
        functools.partial(early_kernel, scale),
        [
            jax.ShapeDtypeStruct((tok_rows, 2 * half), f32),
            jax.ShapeDtypeStruct((tok_rows, HD), f32),
        ],
        "attention_early",
        3 * attn_flops,
        queries,
        key_all,
        value_all,
        query_pos[:, None],
        key_pos[None, :],
    )

    bit = z_index % 2
    stay, leave = expert_block(bit.reshape(1), rows, weights)
    up = [(2 * a, 2 * ((a + 1) % z_count)) for a in range(z_count)]
    down = [(2 * a + 1, 2 * ((a - 1) % z_count) + 1) for a in range(z_count)]
    came = lax.ppermute(leave, ("z", "core"), up + down)
    left = (stay + came.astype(f32)).astype(bf16)
    same = [list(range(r, z_count, 2)) for r in range(2)]
    left = lax.all_to_all(left, "z", 0, 0, tiled=True, axis_index_groups=same)
    left, probs, output, key_all, value_all = lax.optimization_barrier(
        (left, probs, output, key_all, value_all)
    )
    slots = jnp.sum(left.astype(f32), axis=0).astype(bf16)
    slots = lax.all_to_all(
        jnp.broadcast_to(slots[None], (exp_count, *slots.shape)), "exp", 0, 0, tiled=True
    )
    flat = slots.reshape(exp_count * FOLD * CAP, -1)
    pieces = [jnp.dot(there, flat, preferred_element_type=f32) for there in theres]
    summed = jnp.concatenate(pieces, axis=1)
    grad_quarter = norm_back(resid_full, inv_rms, grad_full, norm_gain, summed)

    at_heads = lax.dot_general(grad_quarter, w_four, CONTRACT, preferred_element_type=f32)
    at_heads = at_heads.astype(bf16).reshape(quarter, head_count, HD).transpose(1, 0, 2)
    at_heads = jnp.roll(at_heads, head_index, axis=0)
    attn_grad = lax.all_to_all(at_heads, "head", 0, 0, tiled=True).reshape(tok_rows, HD)
    query_grad = in_vmem(
        functools.partial(late_kernel, scale),
        jax.ShapeDtypeStruct((tok_rows, HD), bf16),
        "attention_late",
        3 * attn_flops,
        attn_grad,
        key_all,
        value_all,
        probs,
        output,
    )
    return (grad_quarter, query_grad)


def solution(mesh):
    seq, exp, head = mesh.shape["seq"], mesh.shape["exp"], mesh.shape["head"]
    fine = Mesh(mesh.devices.reshape(seq // 2, 2, exp, head), ("z", "core", "exp", "head"))
    seq_axes = ("z", "core")
    in_specs = (
        P(seq_axes, None),
        P(seq_axes, None),
        P(),
        P(seq_axes, None),
        P(seq_axes, None),
        P("exp", None, seq_axes),
        P("exp", None, seq_axes),
        P("exp", seq_axes, None),
        P(("exp", "head"), None),
        P(seq_axes, ("exp", "head")),
        P(seq_axes, ("exp", "head")),
        P(seq_axes, ("exp", "head")),
    )
    out_specs = (P(("z", "core", "head"), None), P(seq_axes, ("exp", "head")))
    return jax.shard_map(
        per_device, mesh=fine, in_specs=in_specs, out_specs=out_specs, check_vma=False
    )
```

```python
import functools

import jax
import jax.numpy as jnp
from jax import lax
from jax.experimental import pallas as pl
from jax.experimental.pallas import tpu as pltpu
from jax.sharding import Mesh, PartitionSpec as P

HD = 128
EPSILON = 1e-05
CAP = 12
FOLD = 4
ROOM = 16
UNITS = 256
MIB = 2**20

CONTRACT = (((1,), (1,)), ((), ()))


def across(left, right):
    return lax.dot_general(left, right, CONTRACT, preferred_element_type=jnp.float32)


def two_terms(full):
    high = full.astype(jnp.bfloat16)
    return high, (full - high.astype(jnp.float32)).astype(jnp.bfloat16)


def expert_kernel(bit_ref, rows_ref, w_ref, stay_ref, leave_ref, back_ref):
    step = pl.program_id(0)
    shards, _, width = rows_ref.shape
    part = width // FOLD
    ins = rows_ref[:, :ROOM, :].reshape(shards * ROOM, width)
    grads = rows_ref[:, ROOM:, :].reshape(shards * ROOM, width)
    gate_val = across(ins, w_ref[0, 0])
    up_val = across(ins, w_ref[0, 1])
    hidden_grad = across(grads, w_ref[0, 2])
    sigma = jax.nn.sigmoid(gate_val)
    gate_grad = (hidden_grad * up_val * sigma * (1.0 + gate_val * (1.0 - sigma))).astype(jnp.bfloat16)
    up_grad = (hidden_grad * gate_val * sigma).astype(jnp.bfloat16)
    for q in range(FOLD):
        at = slice(q * part, (q + 1) * part)
        piece = jnp.dot(gate_grad, w_ref[0, 0, :, at], preferred_element_type=jnp.float32)
        piece = piece + jnp.dot(up_grad, w_ref[0, 1, :, at], preferred_element_type=jnp.float32)
        piece = piece.reshape(shards, ROOM, part)

        @pl.when(step == 0)
        def _():
            back_ref[:, :, at] = piece

        @pl.when(step == 1)
        def _():
            back_ref[:, :, at] += piece

    @pl.when(step == 1)
    def _():
        bit = bit_ref[0]

        def folded(shard):
            block = back_ref[shard]
            return jnp.concatenate([block[:CAP, q * part : (q + 1) * part] for q in range(FOLD)], axis=0)

        for k in range(shards // 2):
            stay_ref[k] = folded(2 * k + bit)
            leave_ref[k] = folded(2 * k + 1 - bit).astype(jnp.bfloat16)


def expert_block(bit, rows, weights):
    shards, depth, width = rows.shape
    out = (shards // 2, FOLD * CAP, width // FOLD)
    return pl.pallas_call(
        expert_kernel,
        grid=(2,),
        in_specs=[
            pl.BlockSpec(memory_space=pltpu.SMEM),
            pl.BlockSpec((shards, depth, width), lambda i: (0, 0, 0)),
            pl.BlockSpec((1, 3, UNITS, width), lambda i: (i, 0, 0, 0)),
        ],
        out_specs=[pl.BlockSpec(out, lambda i: (0, 0, 0))] * 2,
        out_shape=[
            jax.ShapeDtypeStruct(out, jnp.float32),
            jax.ShapeDtypeStruct(out, jnp.bfloat16),
        ],
        scratch_shapes=[pltpu.VMEM((shards, ROOM, width), jnp.float32)],
        compiler_params=pltpu.CompilerParams(vmem_limit_bytes=48 * MIB),
        cost_estimate=pl.CostEstimate(
            flops=2 * 5 * shards * ROOM * 2 * UNITS * width,
            bytes_accessed=2 * weights.size + 2 * rows.size,
            transcendentals=0,
        ),
        name="expert_block",
    )(bit, rows, weights)


def early_kernel(scale, query_ref, key_ref, value_ref, qpos_ref, kpos_ref, prob_ref, out_ref):
    allowed = kpos_ref[...] <= qpos_ref[...]
    scores = jnp.where(allowed, across(query_ref[...], key_ref[...]) * scale, -1e30)
    row_max = jnp.max(scores, axis=-1, keepdims=True)
    expo_vals = jnp.where(allowed, jnp.exp(scores - row_max), 0.0)
    probs = expo_vals / jnp.sum(expo_vals, axis=-1, keepdims=True)
    prob_ref[...] = probs
    high, low = two_terms(probs)
    values = value_ref[...]
    out_ref[...] = jnp.dot(high, values, preferred_element_type=jnp.float32) + jnp.dot(
        low, values, preferred_element_type=jnp.float32
    )


def late_kernel(scale, grad_ref, key_ref, value_ref, prob_ref, out_ref, back_ref):
    grads = grad_ref[...]
    delta = jnp.sum(grads.astype(jnp.float32) * out_ref[...], axis=-1, keepdims=True)
    mixed = prob_ref[...] * (across(grads, value_ref[...]) - delta)
    high, low = two_terms(mixed)
    keys = key_ref[...]
    total = jnp.dot(high, keys, preferred_element_type=jnp.float32) + jnp.dot(
        low, keys, preferred_element_type=jnp.float32
    )
    back_ref[...] = (scale * total).astype(jnp.bfloat16)


def in_vmem(kernel, out_shape, name, flops, *args):
    return pl.pallas_call(
        kernel,
        in_specs=[pl.BlockSpec(memory_space=pltpu.VMEM)] * len(args),
        out_specs=jax.tree.map(lambda _: pl.BlockSpec(memory_space=pltpu.VMEM), out_shape),
        out_shape=out_shape,
        compiler_params=pltpu.CompilerParams(vmem_limit_bytes=32 * MIB),
        cost_estimate=pl.CostEstimate(flops=flops, bytes_accessed=4 * MIB, transcendentals=0),
        name=name,
    )(*args)


def core_swap(block):
    return lax.ppermute(block, "core", [(0, 1), (1, 0)])


def norm_back(resid_full, inv_rms, grad_rows, norm_gain, expert_grad):
    scaled_grad = norm_gain.astype(jnp.float32) * expert_grad
    cubed = inv_rms * inv_rms * inv_rms
    mean_term = jnp.mean(scaled_grad * resid_full, axis=-1, keepdims=True)
    return (grad_rows + inv_rms * scaled_grad - resid_full * cubed * mean_term).astype(jnp.bfloat16)


def per_device(
    resid,
    grad_out,
    norm_gain,
    expert_ids,
    route_weights,
    w_gate,
    w_up,
    w_down,
    w_out,
    queries,
    keys,
    values,
):
    f32, bf16 = jnp.float32, jnp.bfloat16
    tok_rows, width = resid.shape
    z_count, exp_count, head_count = (lax.axis_size(a) for a in ("z", "exp", "head"))
    z_index, core_index = lax.axis_index("z"), lax.axis_index("core")
    exp_index, head_index = lax.axis_index("exp"), lax.axis_index("head")
    quarter = tok_rows // head_count
    row_first = head_index * quarter
    resid_part = lax.dynamic_slice_in_dim(resid, row_first, quarter, 0)
    grad_part = lax.dynamic_slice_in_dim(grad_out, row_first, quarter, 0)
    ids_part = lax.dynamic_slice_in_dim(expert_ids, row_first, quarter, 0)
    weights_part = lax.dynamic_slice_in_dim(route_weights, row_first, quarter, 0)
    resid_full = resid_part.astype(f32)
    inv_rms = lax.rsqrt(jnp.mean(resid_full * resid_full, axis=-1, keepdims=True) + EPSILON)
    normed = (resid_full * inv_rms * norm_gain.astype(f32)).astype(bf16)
    grad_full = grad_part.astype(f32)

    row_ids = jnp.arange(quarter, dtype=jnp.int32)
    earlier = row_ids[:, None] < row_ids[None, :]

    def slots_of(expert):
        matched = ids_part == expert
        routed = jnp.any(matched, axis=1)
        position = jnp.sum((earlier & routed[:, None]).astype(jnp.int32), axis=0)
        weight = jnp.sum(jnp.where(matched, weights_part, 0.0), axis=1)
        return routed, position, weight

    routed, position, weight = slots_of(exp_index)
    slot_ids = jnp.arange(ROOM, dtype=jnp.int32)
    select = ((position[None, :] == slot_ids[:CAP, None]) & routed[None, :]).astype(bf16)
    scaled = (weight[:, None] * grad_full).astype(bf16)
    slot_in = jnp.dot(select, normed, preferred_element_type=f32).astype(bf16)
    slot_grad = jnp.dot(select, scaled, preferred_element_type=f32).astype(bf16)
    spare = ROOM - CAP
    mine = jnp.concatenate(
        [slot_in, keys.reshape(spare, -1), slot_grad, values.reshape(spare, -1)], axis=0
    )

    rows = lax.all_gather(mine, "z", axis=0, tiled=True).reshape(z_count, 2 * ROOM, width)
    gate_mat, up_mat, down_mat, w_mine, mine = lax.optimization_barrier(
        (w_gate[0].T, w_up[0].T, w_down[0], w_out, mine)
    )
    fill = ((0, UNITS - gate_mat.shape[0]), (0, 0))
    own = jnp.stack([jnp.pad(w, fill) for w in (gate_mat, up_mat, down_mat)], axis=0)
    weights = jnp.stack([own, core_swap(own)], axis=0)
    w_near = [w_mine] + [
        lax.ppermute(w_mine, "head", [(a, (a - d) % head_count) for a in range(head_count)])
        for d in range(1, head_count)
    ]
    w_four = jnp.concatenate(w_near, axis=0)
    picks = []
    for expert in range(exp_count):
        routed, position, _ = slots_of(expert)
        picks.append((position[:, None] == slot_ids[None, :CAP]) & routed[:, None])
    picks = jnp.stack(picks, axis=1).astype(bf16)
    theres = []
    for q in range(FOLD):
        there = jnp.zeros((quarter, exp_count, FOLD, CAP), bf16).at[:, :, q].set(picks)
        theres.append(there.reshape(quarter, -1))
    weights, w_four, *theres = lax.optimization_barrier((weights, w_four, *theres))

    packed = rows.reshape(z_count, 2, ROOM, width)[:, :, CAP:]
    packed = jnp.stack([packed, core_swap(packed)], axis=0)
    key_all = packed[:, :, 0].reshape(-1, HD)
    value_all = packed[:, :, 1].reshape(-1, HD)
    query_pos = (z_index * 2 + core_index) * tok_rows + jnp.arange(tok_rows, dtype=jnp.int32)
    place = jnp.arange(2 * z_count * tok_rows, dtype=jnp.int32)
    half = z_count * tok_rows
    shard = (place % half) // tok_rows * 2 + (core_index + place // half) % 2
    key_pos = shard * tok_rows + place % tok_rows
    scale = HD ** (-0.5)
    attn_flops = 2 * tok_rows * HD * 2 * half
    probs, output = in_vmem(
        functools.partial(early_kernel, scale),
        [
            jax.ShapeDtypeStruct((tok_rows, 2 * half), f32),
            jax.ShapeDtypeStruct((tok_rows, HD), f32),
        ],
        "attention_early",
        3 * attn_flops,
        queries,
        key_all,
        value_all,
        query_pos[:, None],
        key_pos[None, :],
    )

    bit = z_index % 2
    stay, leave = expert_block(bit.reshape(1), rows, weights)
    up = [(2 * a, 2 * ((a + 1) % z_count)) for a in range(z_count)]
    down = [(2 * a + 1, 2 * ((a - 1) % z_count) + 1) for a in range(z_count)]
    came = lax.ppermute(leave, ("z", "core"), up + down)
    left = (stay + came.astype(f32)).astype(bf16)
    left, probs, output, key_all, value_all = lax.optimization_barrier(
        (left, probs, output, key_all, value_all)
    )
    same = [list(range(r, z_count, 2)) for r in range(2)]
    left = lax.all_to_all(left, "z", 0, 0, tiled=True, axis_index_groups=same)
    slots = jnp.sum(left.astype(f32), axis=0).astype(bf16)
    slots = lax.all_to_all(
        jnp.broadcast_to(slots[None], (exp_count, *slots.shape)), "exp", 0, 0, tiled=True
    )
    flat = slots.reshape(exp_count * FOLD * CAP, -1)
    pieces = [jnp.dot(there, flat, preferred_element_type=f32) for there in theres]
    summed = jnp.concatenate(pieces, axis=1)
    grad_quarter = norm_back(resid_full, inv_rms, grad_full, norm_gain, summed)

    at_heads = lax.dot_general(grad_quarter, w_four, CONTRACT, preferred_element_type=f32)
    at_heads = at_heads.astype(bf16).reshape(quarter, head_count, HD).transpose(1, 0, 2)
    at_heads = jnp.roll(at_heads, head_index, axis=0)
    attn_grad = lax.all_to_all(at_heads, "head", 0, 0, tiled=True).reshape(tok_rows, HD)
    query_grad = in_vmem(
        functools.partial(late_kernel, scale),
        jax.ShapeDtypeStruct((tok_rows, HD), bf16),
        "attention_late",
        3 * attn_flops,
        attn_grad,
        key_all,
        value_all,
        probs,
        output,
    )
    return (grad_quarter, query_grad)


def solution(mesh):
    seq, exp, head = mesh.shape["seq"], mesh.shape["exp"], mesh.shape["head"]
    fine = Mesh(mesh.devices.reshape(seq // 2, 2, exp, head), ("z", "core", "exp", "head"))
    seq_axes = ("z", "core")
    in_specs = (
        P(seq_axes, None),
        P(seq_axes, None),
        P(),
        P(seq_axes, None),
        P(seq_axes, None),
        P("exp", None, seq_axes),
        P("exp", None, seq_axes),
        P("exp", seq_axes, None),
        P(("exp", "head"), None),
        P(seq_axes, ("exp", "head")),
        P(seq_axes, ("exp", "head")),
        P(seq_axes, ("exp", "head")),
    )
    out_specs = (P(("z", "core", "head"), None), P(seq_axes, ("exp", "head")))
    return jax.shard_map(
        per_device, mesh=fine, in_specs=in_specs, out_specs=out_specs, check_vma=False
    )
```
